256 devices in a mesh: layer: 4 (over x), row: 64 (over y, z, core).
Axes of the slice: x: 4, y: 4, z: 8, core: 2. Of those that a mesh axis runs over, the one named last changes fastest.
Arguments:
- tokens: bfloat16 [128, 8192], P('row'), may hold values from -6 to 6
- up_weight: bfloat16 [4, 32768, 8192], P('layer', 'row'), may hold values from -6 to 6
- hess_panel: float32 [4, 256, 8192], P('layer', None, 'row'), may hold values from -1 to 2, as said below
- keep_mask: int32 [4, 32768, 256], P('layer', 'row'), may hold values from 0 to 1, as said below
Outputs:
- section_acts: bfloat16 [4, 128, 8192], P('layer', 'row')
- pruned_blocks: bfloat16 [4, 32768, 256], P('layer', 'row')
The draws below stay inside these ranges and needn't reach their ends.
Inputs may be any that keep to these rules, and one draw needn't show every extreme that they name: `keep_mask`: each row has exactly 64 ones in each block of 128 columns. `hess_panel`: zero where the column is below the row; the diagonal lies in [0.5, 2].
All inputs are finite; a program needn't handle non-finite values.
Results may differ from the reference program's by a relative error of at most 0.017.
Values may be sent and summed in bfloat16 or wider, within the bound.
A program may use at most 192 MiB of HBM per device.

```python
import math
import jax
import jax.numpy as jnp
from jax import lax

D = 8192
FFW = 32768
BLOCK = 128
TOKENS = 128
N_LAYER = 4


def draw_keep_mask(key, part):
    total_rows = N_LAYER * FFW * 2
    row_keys = jax.random.split(key, total_rows)
    orders = jax.vmap(lambda single: jax.random.permutation(single, BLOCK))(row_keys)
    retained = (orders < BLOCK // 2).astype(jnp.int32)
    return retained.reshape(N_LAYER, FFW, 2 * BLOCK)


def draw_hess_panel(key, part):
    key_list = jax.random.split(jax.random.fold_in(key, 17), 4)
    first_key = key_list[0]
    second_key = key_list[1]
    row_key = key_list[2]
    column_key = key_list[3]
    panel_shape = (N_LAYER, 2 * BLOCK, D)
    entries = jnp.clip(jax.random.normal(first_key, panel_shape, jnp.float32), -4.0, 4.0)
    row_index = jnp.arange(2 * BLOCK)[:, None]
    column_index = jnp.arange(D)[None, :]
    factor = jnp.where(column_index < 2 * BLOCK, 0.5 / math.sqrt(BLOCK), 1.0 / math.sqrt(2 * BLOCK))
    row_scale = jax.random.uniform(row_key, (N_LAYER, 2 * BLOCK, 1), jnp.float32, 0.5, 1.5)
    column_scale = jax.random.uniform(column_key, (N_LAYER, 1, D), jnp.float32, 0.5, 1.5)
    coherent = jnp.where(column_index < 2 * BLOCK, 0.08 * row_scale * column_scale, 0.0)
    pivots = jnp.exp(jax.random.uniform(second_key, (N_LAYER, 2 * BLOCK, 1), jnp.float32, math.log(0.5), math.log(2.0)))
    upper = jnp.where(column_index > row_index, entries * factor + coherent, 0.0)
    return (upper + jnp.where(column_index == row_index, pivots, 0.0)).astype(jnp.float32)


def block_levels(stream_key, extent, cuts, smallest, high):
    factor_of = 1.0
    for position, blocks in cuts:
        draws = jax.random.uniform(jax.random.fold_in(jax.random.fold_in(stream_key, 6), position), (blocks,), jnp.float32, smallest / len(cuts), high / len(cuts))
        factor_of = factor_of * jnp.repeat(jnp.exp(draws), extent[position] // blocks).reshape((-1,) + (1,) * (len(extent) - 1 - position))
    return factor_of


def normal_values(rng, extent, spread, bound, cuts=(), held_as=jnp.bfloat16):
    level = block_levels(rng, extent, cuts, -0.22, 0.18) if cuts else 1.0
    values = jax.random.normal(rng, extent, jnp.float32) * spread * level
    return jnp.minimum(jnp.maximum(values, -bound), bound).astype(held_as)


def setup_inputs(seed: int = 0) -> dict:
    streams_of = jax.random.split(jax.random.key(seed), 5)
    tokens = normal_values(streams_of[0], (TOKENS, D), 1.0, 6.0, ((0, 64),))
    up_weight = normal_values(streams_of[1], (N_LAYER, FFW, D), 1.0, 6.0, ((0, 4), (1, 64)))
    hess_panel = draw_hess_panel(jax.random.fold_in(streams_of[4], 71), 0)
    keep_mask = draw_keep_mask(jax.random.fold_in(streams_of[4], 71), 0)
    return dict(tokens=tokens, up_weight=up_weight, hess_panel=hess_panel, keep_mask=keep_mask)


epsilon = 1e-05

def highest_dot(left, right):
    return jnp.dot(left, right, precision=lax.Precision.HIGHEST, preferred_element_type=jnp.float32)

def eliminate(columns_in, pivot_block, retained):
    count = pivot_block.shape[0]
    width_sub = min(16, count)
    inverse = 1.0 / jnp.diagonal(pivot_block)
    dropped = 1.0 - retained.astype(jnp.float32)
    residual = columns_in
    error_list = []
    for start in range(0, count, width_sub):
        finish = start + width_sub
        current = residual[:, start:finish]
        local_errors = []
        for offset in range(width_sub):
            index_col = start + offset
            error = current[:, offset:offset + 1] * dropped[:, index_col:index_col + 1] * inverse[index_col]
            current = current - error * pivot_block[index_col:index_col + 1, start:finish]
            local_errors.append(error)
        sub_errors = jnp.concatenate(local_errors, 1)
        error_list.append(sub_errors)
        pieces = [residual[:, :start], current]
        if finish < count:
            pieces.append(residual[:, finish:] - highest_dot(sub_errors, pivot_block[start:finish, finish:]))
        residual = jnp.concatenate(pieces, 1)
    return (residual, jnp.concatenate(error_list, 1))

def prune_layer(weight, panel, retained):
    width_block = panel.shape[0] // 2
    leading = weight[:, :2 * width_block].astype(jnp.float32)
    first_values, errors_first = eliminate(leading[:, :width_block], panel[:width_block, :width_block], retained[:, :width_block])
    second_in = leading[:, width_block:] - highest_dot(errors_first, panel[:width_block, width_block:2 * width_block])
    second_values, errors_second = eliminate(second_in, panel[width_block:, width_block:2 * width_block], retained[:, width_block:])
    pruned = jnp.concatenate([first_values, second_values], 1).astype(jnp.bfloat16)
    return (pruned, jnp.concatenate([errors_first, errors_second], 1))

def advance(inputs, mixed_weight, remote_panel, errors):
    features = inputs.shape[1]
    leading_count = errors.shape[1]
    product = lax.dot_general(inputs, mixed_weight, (((1,), (1,)), ((), ())), preferred_element_type=jnp.float32)
    panel_inputs = lax.dot_general(inputs[:, leading_count:].astype(jnp.float32), remote_panel, (((1,), (1,)), ((), ())), precision=lax.Precision.HIGHEST, preferred_element_type=jnp.float32)
    correction = lax.dot_general(panel_inputs, errors, (((1,), (1,)), ((), ())), precision=lax.Precision.HIGHEST, preferred_element_type=jnp.float32)
    layer_output = ((product - correction) * features ** (-0.5)).astype(jnp.bfloat16)
    hidden = jax.nn.silu(layer_output.astype(jnp.float32))
    folded = hidden.reshape(inputs.shape[0], -1, features).sum(axis=1)
    combined = inputs.astype(jnp.float32) + folded
    moment = lax.optimization_barrier(jnp.mean(combined * combined, axis=-1, keepdims=True))
    return (combined * lax.rsqrt(moment + epsilon)).astype(jnp.bfloat16)

def reference(tokens, up_weight, hess_panel, keep_mask):
    inputs = tokens
    activations = []
    pruned_list = []
    leading_count = 2 * BLOCK
    for layer_index in range(N_LAYER):
        weight = up_weight[layer_index]
        panel = hess_panel[layer_index]
        pruned, errors = prune_layer(weight, panel[:, :leading_count], keep_mask[layer_index])
        mixed_weight = jnp.concatenate([pruned, weight[:, leading_count:]], 1)
        inputs = advance(inputs, mixed_weight, panel[:, leading_count:], errors)
        activations.append(inputs)
        pruned_list.append(pruned)
    return (jnp.stack(activations), jnp.stack(pruned_list))
```

```python
import functools

import jax
import jax.numpy as jnp
from jax import lax
from jax.experimental import pallas as pl
from jax.experimental.pallas import tpu as pltpu
from jax.sharding import PartitionSpec as P

MESH = pl.DeviceIdType.MESH
BF16 = jnp.bfloat16
F32 = jnp.float32

BLOCK = 128
LEAD = 2 * BLOCK
DEPTH = 4
NY = 4
NZ = 8
LINE = 2 * NZ
FEATURES = 8192
UNITS = 512
TOKENS = 128
QUARTER = TOKENS // NY
PAIR = 2
epsilon = 1e-05

DOWN = 2.0**-32
UP = 2.0**32


def position():
    layer = lax.axis_index("layer")
    row = lax.axis_index("row")
    return layer, row // LINE, (row // 2) % NZ, row % 2


def device(layer, y, z, core):
    return (layer, (y * NZ + z) * 2 + core)


def meet(partners):
    barrier = pltpu.get_barrier_semaphore()
    for partner in partners:
        pl.semaphore_signal(barrier, inc=1, device_id=partner, device_id_type=MESH)
    pl.semaphore_wait(barrier, len(partners))


def remote(src, dst, send_sem, recv_sem, target):
    return pltpu.make_async_remote_copy(
        src_ref=src,
        dst_ref=dst,
        send_sem=send_sem,
        recv_sem=recv_sem,
        device_id=target,
        device_id_type=MESH,
    )


OFFSETS = [0, -1, 1, -2, 2, -3, 3, -4]


def offset_of(k):
    return jnp.where(k % 2 == 1, -((k + 1) // 2), k // 2)


def gather(here, block, line, sems, ready):
    layer, y, z, c = here
    zsend, zrecv, ysend, yrecv, csend, crecv = sems
    s = 1 - 2 * c
    other = 1 - c
    wrap_z = lambda v: (v + NZ) % NZ
    wrap_y = lambda v: (v + NY) % NY
    zf = device(layer, y, wrap_z(z + s), c)
    zb = device(layer, y, wrap_z(z - s), c)
    yf = device(layer, wrap_y(y + s), z, c)
    yb = device(layer, wrap_y(y - s), z, c)
    sibling = device(layer, y, z, other)
    y_from, y_to, y_far = wrap_y(y - s), wrap_y(y + s), wrap_y(y + 2)
    started = []

    def send(view, target, ssem, rsem):
        copy = remote(view, view, ssem, rsem, target)
        copy.start()
        started.append(copy)

    def arrive(view, source, ssem, rsem):
        remote(view, view, ssem, rsem, source).wait_recv()

    def along_y(k):
        view = block(y, wrap_z(z + s * OFFSETS[k]), c)
        send(view, yf, ysend.at[k], yrecv.at[k])
        send(view, yb, ysend.at[8 + k], yrecv.at[8 + k])

    def pass_on(k):
        view = block(y_from, wrap_z(z + s * OFFSETS[k]), c)
        arrive(view, yb, ysend.at[k], yrecv.at[k])
        send(view, yf, ysend.at[16 + k], yrecv.at[16 + k])

    own = block(y, z, c)
    send(own, zf, zsend.at[0], zrecv.at[0])
    send(own, zb, zsend.at[4], zrecv.at[4])
    along_y(0)
    for d in range(1, 5):
        view = block(y, wrap_z(z - s * d), c)
        arrive(view, zb, zsend.at[d - 1], zrecv.at[d - 1])
        if d < 4:
            send(view, zf, zsend.at[d], zrecv.at[d])
        along_y(2 * d - 1)
        if d < 4:
            view = block(y, wrap_z(z + s * d), c)
            arrive(view, zf, zsend.at[3 + d], zrecv.at[3 + d])
            if d < 3:
                send(view, zb, zsend.at[4 + d], zrecv.at[4 + d])
            along_y(2 * d)
        if d == 1:
            pass_on(0)
        else:
            pass_on(2 * d - 3)
            pass_on(2 * d - 2)
    send(line(y, c), sibling, csend.at[0], crecv.at[0])
    pass_on(7)
    send(line(y_from, c), sibling, csend.at[1], crecv.at[1])
    for k in range(8):
        arrive(block(y_to, wrap_z(z + s * OFFSETS[k]), c), yf, ysend.at[8 + k], yrecv.at[8 + k])
    send(line(y_to, c), sibling, csend.at[2], crecv.at[2])
    arrive(line(y, other), sibling, csend.at[0], crecv.at[0])
    arrive(line(y_to, other), sibling, csend.at[1], crecv.at[1])
    arrive(line(y_from, other), sibling, csend.at[2], crecv.at[2])

    def last(k, carry):
        zk = wrap_z(z + s * offset_of(k))
        view = block(y_far, zk, c)
        arrive(view, yb, ysend.at[16 + k], yrecv.at[16 + k])
        remote(view, view, csend.at[3 + k], crecv.at[3 + k], sibling).start()
        ready(zk, c)
        zo = wrap_z(z - s * offset_of(k))
        arrive(block(y_far, zo, other), sibling, csend.at[3 + k], crecv.at[3 + k])
        ready(zo, other)
        return carry

    lax.fori_loop(0, 8, last, 0)

    def last_sent(k, carry):
        view = block(y_far, wrap_z(z + s * offset_of(k)), c)
        remote(view, view, csend.at[3 + k], crecv.at[3 + k], sibling).wait_send()
        return carry

    lax.fori_loop(0, 8, last_sent, 0)
    for copy in started:
        copy.wait_send()


GATHER_SEMS = [
    pltpu.SemaphoreType.DMA((7,)),
    pltpu.SemaphoreType.DMA((7,)),
    pltpu.SemaphoreType.DMA((24,)),
    pltpu.SemaphoreType.DMA((24,)),
    pltpu.SemaphoreType.DMA((11,)),
    pltpu.SemaphoreType.DMA((11,)),
]


def ring_partners(here):
    layer, y, z, c = here
    return [
        device(layer, y, (z + 1) % NZ, c),
        device(layer, y, (z + NZ - 1) % NZ, c),
        device(layer, (y + 1) % NY, z, c),
        device(layer, (y + NY - 1) % NY, z, c),
        device(layer, y, z, 1 - c),
    ]


def panel_kernel(panel_ref, full_ref, *sems):
    here = position()
    _, y, z, c = here
    meet(ring_partners(here))
    full_ref[y * NZ + z, c] = panel_ref[...].astype(BF16)
    gather(
        here,
        lambda yy, zz, cc: full_ref.at[yy * NZ + zz, cc],
        lambda yy, cc: full_ref.at[pl.ds(yy * NZ, NZ), cc],
        sems,
        lambda zz, cc: None,
    )


def gather_panel(panel):
    rows, columns = panel.shape
    return pl.pallas_call(
        panel_kernel,
        out_shape=jax.ShapeDtypeStruct((NY * NZ, 2, rows, columns), BF16),
        in_specs=[pl.BlockSpec(memory_space=pltpu.VMEM)],
        out_specs=pl.BlockSpec(memory_space=pltpu.VMEM),
        scratch_shapes=GATHER_SEMS,
        compiler_params=pltpu.CompilerParams(
            collective_id=0, has_side_effects=True, vmem_limit_bytes=24 * 2**20
        ),
        name="gather_panel",
    )(panel)


SUB = 16


def eliminate_kernel(weight_ref, mask_ref, factor_ref, pruned_ref, errors_ref, scaled_ref):
    work = weight_ref[...].astype(F32).T
    first, second = factor_ref[0, 0].astype(F32), factor_ref[0, 1].astype(F32)
    eye = (
        lax.broadcasted_iota(jnp.int32, (BLOCK, BLOCK), 0)
        == lax.broadcasted_iota(jnp.int32, (BLOCK, BLOCK), 1)
    )
    diagonal = jnp.concatenate(
        [
            jnp.sum(jnp.where(eye, first[:BLOCK], 0.0), axis=1, keepdims=True),
            jnp.sum(jnp.where(eye, second[BLOCK:], 0.0), axis=1, keepdims=True),
        ],
        0,
    )
    dropped = 1.0 - mask_ref[...].astype(F32).T
    scaled_ref[...] = dropped * (1.0 / diagonal)
    turned = jnp.concatenate([first.T, second.T], 0)
    turned16 = turned.astype(BF16)
    count = LEAD // SUB
    finished = []
    high, low = [], []
    window = work[: 2 * SUB]
    for g in range(count):
        start = g * SUB
        final = g + 1 == count
        rows = SUB if final else 2 * SUB
        current = window[:rows]
        following = None
        if g + 2 < count:
            following = work[start + 2 * SUB : start + 3 * SUB]
            if g > 0:
                part = turned16[start + 2 * SUB : start + 3 * SUB, :start]
                following = (
                    following
                    - jnp.dot(part, jnp.concatenate(high, 0), preferred_element_type=F32)
                    - jnp.dot(part, jnp.concatenate(low, 0), preferred_element_type=F32)
                )
        local = []
        for o in range(SUB):
            j = start + o
            error = current[o : o + 1] * scaled_ref[j : j + 1, :]
            current = current - turned[start : start + rows, j : j + 1] * error
            local.append(error)
        errors = jnp.concatenate(local, 0)
        errors_high = errors.astype(BF16)
        errors_low = (errors - errors_high.astype(F32)).astype(BF16)
        high.append(errors_high)
        low.append(errors_low)
        finished.append(current[:SUB])
        if not final:
            window = current[SUB:]
            if following is not None:
                part = turned16[start + 2 * SUB : start + 3 * SUB, start : start + SUB]
                following = (
                    following
                    - jnp.dot(part, errors_high, preferred_element_type=F32)
                    - jnp.dot(part, errors_low, preferred_element_type=F32)
                )
                window = jnp.concatenate([window, following], 0)
    pruned_ref[...] = jnp.concatenate(finished, 0).T.astype(BF16)
    errors_ref[0] = jnp.concatenate(high, 0)
    errors_ref[1] = jnp.concatenate(low, 0)


def eliminate(weight, mask, factor):
    return pl.pallas_call(
        eliminate_kernel,
        grid=(1,),
        out_shape=(
            jax.ShapeDtypeStruct((UNITS, LEAD), BF16),
            jax.ShapeDtypeStruct((2, LEAD, UNITS), BF16),
        ),
        in_specs=[
            pl.BlockSpec((UNITS, LEAD), lambda i: (0, 0)),
            pl.BlockSpec((UNITS, LEAD), lambda i: (0, 0)),
            pl.BlockSpec((1, 2, LEAD, BLOCK), lambda i: (0, 0, 0, 0)),
        ],
        out_specs=(
            pl.BlockSpec((UNITS, LEAD), lambda i: (0, 0)),
            pl.BlockSpec((2, LEAD, UNITS), lambda i: (0, 0, 0)),
        ),
        scratch_shapes=[pltpu.VMEM((LEAD, UNITS), F32)],
        compiler_params=pltpu.CompilerParams(vmem_limit_bytes=32 * 2**20),
        name="eliminate",
    )(weight, mask, factor)


def exchange_line(here, pieces, landed, send_sems, recv_sems):
    layer, y, z, c = here
    me = 2 * z + c

    def message(i):
        peer = (me + i) % LINE
        return remote(
            pieces.at[peer],
            landed.at[me],
            send_sems.at[i],
            recv_sems.at[i],
            device(layer, y, peer // 2, peer % 2),
        )

    def start(i, carry):
        message(i).start()
        return carry

    def wait(i, carry):
        source = (me + LINE - i) % LINE
        remote(
            pieces.at[source],
            landed.at[source],
            send_sems.at[i],
            recv_sems.at[i],
            device(layer, y, source // 2, source % 2),
        ).wait_recv()
        message(i).wait_send()
        return carry

    lax.fori_loop(1, LINE, start, 0)
    landed[me] = pieces[me]
    lax.fori_loop(1, LINE, wait, 0)


def silu(v):
    return v / (1.0 + jnp.exp(-v))


def forward_kernel(
    tokens_ref,
    weight_ref,
    pruned_ref,
    errors_ref,
    panel_ref,
    acts_ref,
    x_ref,
    w_ref,
    u_ref,
    total_ref,
    squares_ref,
    scale_ref,
    out_ref,
    spread_ref,
    hand_ref,
    hold_ref,
    pieces_ref,
    landed_ref,
    pieces2_ref,
    landed2_ref,
    load_sems,
    token_send,
    token_recv,
    act_send,
    act_recv,
    spread_send,
    spread_recv,
    hand_send,
    hand_recv,
    *sems,
):
    here = position()
    layer, y, z, c = here
    me = 2 * z + c
    width = FEATURES // LINE

    loads = [
        pltpu.make_async_copy(pruned_ref, w_ref.at[0, :, pl.ds(0, LEAD)], load_sems.at[0]),
        pltpu.make_async_copy(
            weight_ref.at[:, pl.ds(LEAD, width - LEAD)],
            w_ref.at[0, :, pl.ds(LEAD, width - LEAD)],
            load_sems.at[1],
        ),
        pltpu.make_async_copy(panel_ref, u_ref, load_sems.at[2]),
    ]
    for k in range(1, LINE):
        loads.append(
            pltpu.make_async_copy(
                weight_ref.at[:, pl.ds(k * width, width)], w_ref.at[k], load_sems.at[2 + k]
            )
        )
    for load in loads:
        load.start()

    partners = [device(layer, y, ((me + i) % LINE) // 2, (me + i) % 2) for i in range(1, LINE)]
    partners += [device(layer, (y + i) % NY, z, c) for i in range(1, NY)]
    partners += [device((layer + i) % DEPTH, y, z, c) for i in (1, DEPTH - 1)]
    meet(partners)

    def block(yy, zz, cc):
        return x_ref.at[zz, cc, pl.ds(pl.multiple_of(yy * QUARTER, QUARTER), QUARTER), :]

    def hand_on(target):
        return remote(hand_ref, block(y, z, c), hand_send, hand_recv, target)

    @pl.when(layer == 0)
    def _():
        tokens = tokens_ref[...].astype(F32)
        for p in range(LINE):
            for b in range(4):
                at = p * width + b * 128
                pieces_ref[p, PAIR * b : PAIR * (b + 1), :] = tokens[:, at : at + 128]
        exchange_line(here, pieces_ref, landed_ref, token_send, token_recv)
        for p in range(LINE):
            for b in range(4):
                hold_ref[PAIR * p : PAIR * (p + 1), b * 128 : (b + 1) * 128] = landed_ref[
                    p, PAIR * b : PAIR * (b + 1), :
                ]
        x_ref[z, c, pl.ds(pl.multiple_of(y * QUARTER, QUARTER), QUARTER), :] = hold_ref[...].astype(BF16)

    @pl.when(layer > 0)
    def _():
        hand_on(device((layer + DEPTH - 1) % DEPTH, y, z, c)).wait_recv()

    total_ref[...] = jnp.zeros_like(total_ref)
    squares_ref[...] = jnp.zeros_like(squares_ref)
    for load in loads:
        load.wait()
    u_ref[0] = jnp.zeros_like(u_ref[0])

    def ready(zz, cc):
        k = 2 * zz + cc
        x = x_ref[zz, cc]
        product = lax.dot_general(x, w_ref[k], (((1,), (1,)), ((), ())), preferred_element_type=F32)
        factor = jnp.concatenate(
            [u_ref[2 * k, 0], u_ref[2 * k, 1], u_ref[2 * k + 1, 0], u_ref[2 * k + 1, 1]], 1
        )
        inputs = lax.dot_general(x, factor, (((1,), (1,)), ((), ())), preferred_element_type=F32)
        total_ref[:, :UNITS] += product
        total_ref[:, UNITS:] += inputs
        wide = x.astype(F32)
        wide = wide * wide
        squares_ref[...] += wide[:, :128] + wide[:, 128:256] + wide[:, 256:384] + wide[:, 384:]

    gather(
        here,
        block,
        lambda yy, cc: x_ref.at[:, cc, pl.ds(pl.multiple_of(yy * QUARTER, QUARTER), QUARTER), :],
        sems,
        ready,
    )

    moment = jnp.sum(squares_ref[...], axis=1, keepdims=True) * (UP * UP / FEATURES)
    scale = jnp.where(layer == 0, 1.0, lax.rsqrt(moment + epsilon) * UP)
    scale_ref[...] = jnp.broadcast_to(scale, scale_ref.shape)
    inputs = total_ref[:, UNITS:]
    inputs_high = inputs.astype(BF16)
    inputs_low = (inputs - inputs_high.astype(F32)).astype(BF16)
    correction = (
        jnp.dot(inputs_high, errors_ref[0], preferred_element_type=F32)
        + jnp.dot(inputs_low, errors_ref[0], preferred_element_type=F32)
        + jnp.dot(inputs_high, errors_ref[1], preferred_element_type=F32)
    )
    output = ((total_ref[:, :UNITS] - correction) * (scale * FEATURES**-0.5)).astype(BF16)
    for q in range(NY):
        out_ref[q] = output[q * QUARTER : (q + 1) * QUARTER]

    spreads = []
    for i in range(1, NY):
        q = (y + i) % NY
        copy = remote(
            out_ref.at[q], spread_ref.at[y], spread_send.at[i], spread_recv.at[i], device(layer, q, z, c)
        )
        copy.start()
        spreads.append(copy)
    spread_ref[y] = out_ref[y]
    rows = pl.ds(pl.multiple_of(y * QUARTER, QUARTER), QUARTER)
    residual = x_ref[z, c, rows, :].astype(F32) * scale_ref[rows, :1]
    for i in range(1, NY):
        q = (y + NY - i) % NY
        remote(
            out_ref.at[q], spread_ref.at[q], spread_send.at[i], spread_recv.at[i], device(layer, q, z, c)
        ).wait_recv()
    folded = (
        silu(spread_ref[0].astype(F32))
        + silu(spread_ref[1].astype(F32))
        + silu(spread_ref[2].astype(F32))
        + silu(spread_ref[3].astype(F32))
    )
    combined = residual + folded
    following = device((layer + 1) % DEPTH, y, z, c)

    @pl.when(layer < DEPTH - 1)
    def _():
        hand_ref[...] = (combined * DOWN).astype(BF16)
        hand_on(following).start()

    for p in range(LINE):
        for b in range(4):
            pieces2_ref[p, PAIR * b : PAIR * (b + 1), :] = combined[
                PAIR * p : PAIR * (p + 1), b * 128 : (b + 1) * 128
            ]
    exchange_line(here, pieces2_ref, landed2_ref, act_send, act_recv)
    pair = landed2_ref[...]
    sums = jnp.sum(jnp.sum(pair * pair, axis=0), axis=1, keepdims=True)
    token = lax.broadcasted_iota(jnp.int32, (PAIR * 4, 1), 0) % PAIR
    mean0 = jnp.sum(jnp.where(token == 0, sums, 0.0), axis=0, keepdims=True) * (1.0 / FEATURES)
    mean1 = jnp.sum(jnp.where(token == 1, sums, 0.0), axis=0, keepdims=True) * (1.0 / FEATURES)
    normal = lax.rsqrt(jnp.where(token == 0, mean0, mean1) + epsilon)
    acts = (pair * normal[None]).astype(F32)
    for p in range(LINE):
        for b in range(4):
            at = p * width + b * 128
            acts_ref[:, at : at + 128] = acts[p, PAIR * b : PAIR * (b + 1), :].astype(BF16)

    for copy in spreads:
        copy.wait_send()

    @pl.when(layer < DEPTH - 1)
    def _():
        hand_on(following).wait_send()


def forward(tokens, weight, pruned, errors, panel):
    width = FEATURES // LINE
    vmem = pl.BlockSpec(memory_space=pltpu.VMEM)
    hbm = pl.BlockSpec(memory_space=pl.ANY)
    dma = pltpu.SemaphoreType.DMA
    return pl.pallas_call(
        forward_kernel,
        out_shape=jax.ShapeDtypeStruct((PAIR, FEATURES), BF16),
        in_specs=[vmem, hbm, hbm, vmem, hbm],
        out_specs=vmem,
        scratch_shapes=[
            pltpu.VMEM((NZ, 2, TOKENS, width), BF16),
            pltpu.VMEM((LINE, UNITS, width), BF16),
            pltpu.VMEM(panel.shape, BF16),
            pltpu.VMEM((TOKENS, UNITS + LEAD), F32),
            pltpu.VMEM((TOKENS, 128), F32),
            pltpu.VMEM((TOKENS, 128), F32),
            pltpu.VMEM((NY, QUARTER, UNITS), BF16),
            pltpu.VMEM((NY, QUARTER, UNITS), BF16),
            pltpu.VMEM((QUARTER, UNITS), BF16),
            pltpu.VMEM((QUARTER, UNITS), F32),
            pltpu.VMEM((LINE, PAIR * 4, 128), F32),
            pltpu.VMEM((LINE, PAIR * 4, 128), F32),
            pltpu.VMEM((LINE, PAIR * 4, 128), F32),
            pltpu.VMEM((LINE, PAIR * 4, 128), F32),
            dma((LINE + 2,)),
            dma((LINE,)),
            dma((LINE,)),
            dma((LINE,)),
            dma((LINE,)),
            dma((NY,)),
            dma((NY,)),
            dma,
            dma,
            *GATHER_SEMS,
        ],
        compiler_params=pltpu.CompilerParams(
            collective_id=1, has_side_effects=True, vmem_limit_bytes=48 * 2**20
        ),
        name="forward",
    )(tokens, weight, pruned, errors, panel)


def per_device(tokens, up_weight, hess_panel, keep_mask):
    weight = up_weight[0]
    panel = gather_panel(hess_panel[0])
    pruned, errors = eliminate(weight, keep_mask[0], panel)
    acts = forward(tokens, weight, pruned, errors, panel)
    return (acts[None], pruned[None])


def solution(mesh):
    in_specs = (
        P("row", None),
        P("layer", "row", None),
        P("layer", None, "row"),
        P("layer", "row", None),
    )
    out_specs = (P("layer", "row", None), P("layer", "row", None))
    return jax.shard_map(
        per_device, mesh=mesh, in_specs=in_specs, out_specs=out_specs, check_vma=False
    )
```

```python
import functools

import jax
import jax.numpy as jnp
from jax import lax
from jax.experimental import pallas as pl
from jax.experimental.pallas import tpu as pltpu
from jax.sharding import PartitionSpec as P

MESH = pl.DeviceIdType.MESH
TRANSPOSED = (((1,), (1,)), ((), ()))
BF16 = jnp.bfloat16
F32 = jnp.float32

BLOCK = 128
LEAD = 2 * BLOCK
DEPTH = 4
NY = 4
NZ = 8
LINE = 2 * NZ
FEATURES = 8192
UNITS = 512
TOKENS = 128
QUARTER = TOKENS // NY
PAIR = 2
epsilon = 1e-05

DOWN = 2.0**-32
UP = 2.0**32


def position():
    layer = lax.axis_index("layer")
    row = lax.axis_index("row")
    return layer, row // LINE, (row // 2) % NZ, row % 2


def device(layer, y, z, core):
    return (layer, (y * NZ + z) * 2 + core)


def meet(partners):
    barrier = pltpu.get_barrier_semaphore()
    for partner in partners:
        pl.semaphore_signal(barrier, inc=1, device_id=partner, device_id_type=MESH)
    pl.semaphore_wait(barrier, len(partners))


def remote(src, dst, send_sem, recv_sem, target):
    return pltpu.make_async_remote_copy(
        src_ref=src,
        dst_ref=dst,
        send_sem=send_sem,
        recv_sem=recv_sem,
        device_id=target,
        device_id_type=MESH,
    )


Z_SLOTS = 8
NEAR = slice(0, 5)
FAR = slice(5, 8)
Y_PLACES = 4
BACK = {1: 2, 2: 1, 3: 3}


def slot_z(z, k):
    s = 1 - 2 * (z % 2)
    return (z + NZ + [0, -1, 1, -2 * s, 2 * s, -3, 3, 4][k]) % NZ


def number(condition):
    return condition.astype(jnp.int32)


def z_slot(z, target):
    odd = z % 2
    d = (target - z + NZ) % NZ
    fixed = number(d == 7) + 2 * number(d == 1) + 5 * number(d == 5) + 6 * number(d == 3) + 7 * number(d == 4)
    return fixed + (4 - odd) * number(d == 2) + (3 + odd) * number(d == 6)


def y_place(y, target):
    d = (target - y + NY) % NY
    return d + number(d == 2) - number(d == 3)


class Gather:
    def __init__(self, here, view, sems):
        self.layer, self.y, self.z, self.c = here
        self.view = view
        self.send_sems, self.recv_sems = sems
        odd = self.z % 2
        self.on, self.two_on, self.back = 1 - 2 * odd, 2 - 4 * odd, 2 * odd - 1
        self.two = {2: 3 + odd, -2: 4 - odd}
        self.behind_in, self.ahead_in = 2 + odd, 3 - odd
        self.behind_slot, self.behind_out = 5 + odd, 4 + odd
        self.ahead_slot, self.ahead_out = 6 - odd, 5 - odd
        self.sent = {0: {}, 1: {}}

    def copy(self, core, src, dst, dy, dz, message):
        src, dst = (self.view(slots, core, places) for slots, places in (src, dst))
        target = device(self.layer, (self.y + dy + NY) % NY, (self.z + dz + NZ) % NZ, core)
        return remote(src, dst, self.send_sems.at[message], self.recv_sems.at[message], target)

    def send(self, core, src, dst, dy, dz, message, name=None):
        self.copy(core, src, dst, dy, dz, message).start()
        self.sent[core][name or message] = lambda: self.copy(core, src, dst, dy, dz, message).wait_send()

    def arrive(self, core, dst, message):
        self.copy(core, dst, dst, 1, 0, message).wait_recv()

    def z_out(self, core, places):
        own = (0, places)
        for dz, message in ((2, 2), (-2, 3)):
            self.send(core, own, (self.two[dz], places), 0, dz, message)
        self.send(core, own, (1, places), 0, 1, 0)
        self.send(core, own, (2, places), 0, -1, 1)

    def z_relay(self, core, places):
        behind, ahead = (3, places), (4, places)
        self.arrive(core, behind, self.behind_in)
        self.send(core, behind, (7, places), 0, self.two_on, 6)
        self.send(core, behind, (self.behind_slot, places), 0, self.on, self.behind_out, "behind")
        self.arrive(core, ahead, self.ahead_in)
        self.send(core, ahead, (self.ahead_slot, places), 0, self.back, self.ahead_out, "ahead")

    def z_in(self, core, places, slots):
        for slot in slots:
            self.arrive(core, (slot, places), {1: 0, 2: 1, 5: 4, 6: 5, 7: 6}[slot])

    def y_out(self, core, slots, message):
        own = (slots, 0)
        for place, dy in ((3, 2), (1, 1), (2, -1)):
            self.send(core, own, (slots, BACK[place]), dy, 0, message + place - 1)

    def y_in(self, core, slots, message):
        for place in (1, 2, 3):
            self.arrive(core, (slots, place), message + BACK[place] - 1)

    def other(self, core, slots, message):
        view = self.view(slots, core, slice(0, Y_PLACES))
        target = device(self.layer, self.y, self.z, 1 - self.c)
        return remote(view, view, self.send_sems.at[message], self.recv_sems.at[message], target)

    def to_other(self, core, slots, message):
        self.other(core, slots, message).start()
        self.sent[core][message] = lambda: self.other(core, slots, message).wait_send()

    def from_other(self, slots, message):
        self.other(1 - self.c, slots, message).wait_recv()

    def part(self, core, i):
        every = slice(0, Y_PLACES)
        if core == 0:
            if i == 0:
                self.z_out(core, 0)
                self.y_out(core, 0, 7)
            elif i == 1:
                self.z_relay(core, 0)
                self.z_in(core, 0, (1, 2))
                self.y_out(core, slice(1, 5), 10)
            elif i == 2:
                self.z_in(core, 0, (5, 6, 7))
                self.y_out(core, FAR, 13)
            elif i == 3:
                self.y_in(core, 0, 7)
                self.y_in(core, slice(1, 5), 10)
                self.to_other(core, NEAR, 16)
            else:
                self.y_in(core, FAR, 13)
                self.to_other(core, FAR, 17)
        else:
            if i == 0:
                self.y_out(core, 0, 7)
            elif i == 1:
                self.y_in(core, 0, 7)
                self.z_out(core, every)
            elif i == 2:
                self.z_relay(core, every)
            elif i == 3:
                self.z_in(core, every, (1, 2))
                self.to_other(core, NEAR, 16)
            else:
                self.z_in(core, every, (5, 6, 7))
                self.to_other(core, FAR, 17)

    def finish(self, core):
        for wait in self.sent[core].values():
            wait()


GATHER_SEMS = [pltpu.SemaphoreType.DMA((18,)), pltpu.SemaphoreType.DMA((18,))]


def by_core(c, part):
    for core in (0, 1):
        pl.when(c == core)(functools.partial(part, core))


SUB = 16


def eliminate(weight_ref, mask_ref, factor_ref, pruned_ref, errors_ref, scaled_ref):
    work = weight_ref[...].astype(F32).T
    first, second = factor_ref[0].astype(F32), factor_ref[1].astype(F32)
    eye = (
        lax.broadcasted_iota(jnp.int32, (BLOCK, BLOCK), 0)
        == lax.broadcasted_iota(jnp.int32, (BLOCK, BLOCK), 1)
    )
    diagonal = jnp.concatenate(
        [
            jnp.sum(jnp.where(eye, first[:BLOCK], 0.0), axis=1, keepdims=True),
            jnp.sum(jnp.where(eye, second[BLOCK:], 0.0), axis=1, keepdims=True),
        ],
        0,
    )
    dropped = 1.0 - mask_ref[...].astype(F32).T
    scaled_ref[...] = dropped * (1.0 / diagonal)
    turned = jnp.concatenate([first.T, second.T], 0)
    turned16 = turned.astype(BF16)
    count = LEAD // SUB
    finished = []
    high, low = [], []
    window = work[: 2 * SUB]
    for g in range(count):
        start = g * SUB
        final = g + 1 == count
        rows = SUB if final else 2 * SUB
        current = window[:rows]
        following = None
        if g + 2 < count:
            following = work[start + 2 * SUB : start + 3 * SUB]
            if g > 0:
                part = turned16[start + 2 * SUB : start + 3 * SUB, :start]
                following = (
                    following
                    - jnp.dot(part, jnp.concatenate(high, 0), preferred_element_type=F32)
                    - jnp.dot(part, jnp.concatenate(low, 0), preferred_element_type=F32)
                )
        local = []
        for o in range(SUB):
            j = start + o
            error = current[o : o + 1] * scaled_ref[j : j + 1, :]
            current = current - turned[start : start + rows, j : j + 1] * error
            local.append(error)
        errors = jnp.concatenate(local, 0)
        errors_high = errors.astype(BF16)
        errors_low = (errors - errors_high.astype(F32)).astype(BF16)
        high.append(errors_high)
        low.append(errors_low)
        finished.append(current[:SUB])
        if not final:
            window = current[SUB:]
            if following is not None:
                part = turned16[start + 2 * SUB : start + 3 * SUB, start : start + SUB]
                following = (
                    following
                    - jnp.dot(part, errors_high, preferred_element_type=F32)
                    - jnp.dot(part, errors_low, preferred_element_type=F32)
                )
                window = jnp.concatenate([window, following], 0)
    pruned_ref[...] = jnp.concatenate(finished, 0).T.astype(BF16)
    errors_ref[0] = jnp.concatenate(high, 0)
    errors_ref[1] = jnp.concatenate(low, 0)


def exchange_line(here, pieces, landed, send_sems, recv_sems):
    layer, y, z, c = here
    me = 2 * z + c

    def message(i):
        peer = (me + i) % LINE
        return remote(
            pieces.at[peer],
            landed.at[me],
            send_sems.at[i],
            recv_sems.at[i],
            device(layer, y, peer // 2, peer % 2),
        )

    def start(i, carry):
        message(i).start()
        return carry

    def wait(i, carry):
        source = (me + LINE - i) % LINE
        remote(
            pieces.at[source],
            landed.at[source],
            send_sems.at[i],
            recv_sems.at[i],
            device(layer, y, source // 2, source % 2),
        ).wait_recv()
        message(i).wait_send()
        return carry

    lax.fori_loop(1, LINE, start, 0)
    landed[me] = pieces[me]
    return lambda: lax.fori_loop(1, LINE, wait, 0)


def silu(v):
    return v / (1.0 + jnp.exp(-v))


def forward_kernel(
    tokens_hbm,
    weight_ref,
    panel_hbm,
    mask_hbm,
    acts_ref,
    pruned_ref,
    tokens_ref,
    panel_ref,
    mask_ref,
    leading_ref,
    lead_ref,
    scaled_ref,
    errors_ref,
    x_ref,
    w_ref,
    u_ref,
    total_ref,
    squares_ref,
    out_ref,
    spread_ref,
    hand_ref,
    pieces_ref,
    landed_ref,
    pieces2_ref,
    landed2_ref,
    load_sems,
    lead_send,
    lead_recv,
    token_send,
    token_recv,
    act_send,
    act_recv,
    spread_send,
    spread_recv,
    hand_send,
    hand_recv,
    *sems,
):
    here = position()
    layer, y, z, c = here
    me = 2 * z + c
    width = FEATURES // LINE

    loads = [
        pltpu.make_async_copy(panel_hbm, panel_ref, load_sems.at[0]),
        pltpu.make_async_copy(tokens_hbm, tokens_ref, load_sems.at[1]),
        pltpu.make_async_copy(mask_hbm, mask_ref, load_sems.at[2]),
        pltpu.make_async_copy(weight_ref.at[:, pl.ds(0, LEAD)], leading_ref, load_sems.at[3]),
        pltpu.make_async_copy(
            weight_ref.at[:, pl.ds(LEAD, width - LEAD)],
            w_ref.at[0, :, pl.ds(LEAD, width - LEAD)],
            load_sems.at[4],
        ),
    ]
    for k in range(1, LINE):
        loads.append(
            pltpu.make_async_copy(
                weight_ref.at[:, pl.ds(k * width, width)], w_ref.at[k], load_sems.at[4 + k]
            )
        )
    for load in loads:
        load.start()

    partners = [device(layer, y, ((me + i) % LINE) // 2, (me + i) % 2) for i in range(1, LINE)]
    partners += [device(layer, (y + i) % NY, z, c) for i in range(1, NY)]
    partners += [device((layer + i) % DEPTH, y, z, c) for i in (1, DEPTH - 1)]
    meet(partners)

    def x_view(slots, core, places):
        rows = slice(places.start * QUARTER, places.stop * QUARTER) if isinstance(places, slice) else (
            pl.ds(places * QUARTER, QUARTER)
        )
        return x_ref.at[slots, core, rows, :]

    activations = Gather(here, x_view, sems[:2])
    factor = Gather(here, lambda slots, core, places: u_ref.at[slots, core, places], sems[2:])

    loads[0].wait()
    mine = panel_ref[...].astype(BF16)
    source = (y == 0) & (z == 0)
    u_ref[0, c, 0] = jnp.where(source, 0.0, panel_ref[...]).astype(BF16)

    def lead_copy(core, target, message):
        return remote(lead_ref.at[core], lead_ref.at[core], lead_send.at[message], lead_recv.at[message], target)

    def lead_z(i):
        return lead_copy(c, device(layer, 0, i, c), i)

    def lead_y(i):
        return lead_copy(c, device(layer, i, z, c), 7 + i)

    def lead_other(core):
        return lead_copy(core, device(layer, y, z, 1 - c), 11)

    @pl.when(source)
    def _():
        lead_ref[c] = mine
        for i in (4, 3, 5, 2, 6, 1, 7):
            lead_z(i).start()

    @pl.when(layer == 0)
    def _():
        loads[1].wait()
        tokens = tokens_ref[...].astype(F32)
        for p in range(LINE):
            for b in range(4):
                at = p * width + b * 128
                pieces_ref[p, PAIR * b : PAIR * (b + 1), :] = tokens[:, at : at + 128]

    by_core(c, lambda core: factor.part(core, 0))

    @pl.when((y == 0) & (z > 0))
    def _():
        lead_copy(c, device(layer, 0, 0, c), z).wait_recv()

    @pl.when(y == 0)
    def _():
        for i in (2, 1, 3):
            lead_y(i).start()

    @pl.when(layer == 0)
    def _():
        wait_tokens = exchange_line(here, pieces_ref, landed_ref, token_send, token_recv)
        wait_tokens()
        for p in range(LINE):
            for b in range(4):
                total_ref[PAIR * p : PAIR * (p + 1), b * 128 : (b + 1) * 128] = landed_ref[
                    p, PAIR * b : PAIR * (b + 1), :
                ]
        x_ref[0, c, :QUARTER, :] = total_ref[:QUARTER, :UNITS].astype(BF16)

    pl.when(layer == 0)(lambda: by_core(c, lambda core: activations.part(core, 0)))

    @pl.when(y > 0)
    def _():
        lead_copy(c, device(layer, 0, z, c), 7 + y).wait_recv()

    lead_other(c).start()
    for load in loads[2:4]:
        load.wait()
    lead_other(1 - c).wait_recv()
    eliminate(leading_ref, mask_ref, lead_ref, pruned_ref, errors_ref, scaled_ref)

    @pl.when(layer > 0)
    def _():
        loads[1].wait()

    for load in loads[4:]:
        load.wait()
    w_ref[0, :, :LEAD] = pruned_ref[...]
    total_ref[...] = jnp.zeros_like(total_ref)
    squares_ref[...] = jnp.zeros_like(squares_ref)

    def factor_and_tokens(core):
        for i in range(1, 5):
            if i < 4:
                activations.part(core, i)
            factor.part(core, i)

    def factor_alone(core):
        for i in range(1, 5):
            factor.part(core, i)

    def hand_on(target):
        return remote(hand_ref, x_ref.at[0, c, pl.ds(0, QUARTER), :], hand_send, hand_recv, target)

    pl.when(layer == 0)(lambda: by_core(c, factor_and_tokens))
    pl.when(layer > 0)(lambda: by_core(c, factor_alone))
    factor.from_other(NEAR, 16)
    factor.from_other(FAR, 17)

    @pl.when(layer > 0)
    def _():
        hand_on(device((layer + DEPTH - 1) % DEPTH, y, z, c)).wait_recv()

        def near_activations(core):
            for i in range(4):
                activations.part(core, i)

        by_core(c, near_activations)

    def multiply(slots, core):
        products, inputs, squares = None, None, None
        for slot in slots:
            k = 2 * slot_z(z, slot) + core
            x = x_ref[slot, core]
            place = y_place(y, k // 4)
            sides = [z_slot(z, 2 * (k % 4)), z_slot(z, 2 * (k % 4) + 1)]
            columns = jnp.concatenate([u_ref[sides[j // 2], j % 2, place] for j in range(4)], 1)
            product = lax.dot_general(x, w_ref[k], TRANSPOSED, preferred_element_type=F32)
            entry = lax.dot_general(x, columns, TRANSPOSED, preferred_element_type=F32)
            wide = x.astype(F32)
            wide = wide * wide
            square = wide[:, :128] + wide[:, 128:256] + wide[:, 256:384] + wide[:, 384:]
            if products is None:
                products, inputs, squares = product, entry, square
            else:
                products, inputs, squares = products + product, inputs + entry, squares + square
        total_ref[:, :UNITS] += products
        total_ref[:, UNITS:] += inputs
        squares_ref[...] += squares

    def both(slots, message):
        numbers = range(slots.start, slots.stop)

        def one(i, carry):
            @pl.when(i == 1)
            def _():
                activations.from_other(slots, message)

            multiply(numbers, c + i * (1 - 2 * c))
            return carry

        lax.fori_loop(0, 2, one, 0)

    both(NEAR, 16)
    by_core(c, lambda core: activations.part(core, 4))
    both(FAR, 17)

    moment = jnp.sum(squares_ref[...], axis=1, keepdims=True) * (UP * UP / FEATURES)
    scale = jnp.where(layer == 0, 1.0, lax.rsqrt(moment + epsilon) * UP)
    inputs = total_ref[:, UNITS:]
    inputs_high = inputs.astype(BF16)
    inputs_low = (inputs - inputs_high.astype(F32)).astype(BF16)
    correction = (
        jnp.dot(inputs_high, errors_ref[0], preferred_element_type=F32)
        + jnp.dot(inputs_low, errors_ref[0], preferred_element_type=F32)
        + jnp.dot(inputs_high, errors_ref[1], preferred_element_type=F32)
    )
    output = ((total_ref[:, :UNITS] - correction) * (scale * FEATURES**-0.5)).astype(BF16)
    for place in range(NY):
        out_ref[place] = output[place * QUARTER : (place + 1) * QUARTER]

    def spread(place):
        dy = {1: 1, 2: NY - 1, 3: 2}[place]
        return remote(
            out_ref.at[place],
            spread_ref.at[BACK[place]],
            spread_send.at[place],
            spread_recv.at[BACK[place]],
            device(layer, (y + dy) % NY, z, c),
        )

    for place in (3, 1, 2):
        spread(place).start()
    residual = x_ref[0, c, :QUARTER, :].astype(F32) * scale[:QUARTER]
    combined = residual + silu(out_ref[0].astype(F32))
    for place in (1, 2, 3):
        spread(BACK[place]).wait_recv()
        combined = combined + silu(spread_ref[place].astype(F32))
    following = device((layer + 1) % DEPTH, y, z, c)

    @pl.when(layer < DEPTH - 1)
    def _():
        hand_ref[...] = (combined * DOWN).astype(BF16)
        hand_on(following).start()

    for p in range(LINE):
        for b in range(4):
            pieces2_ref[p, PAIR * b : PAIR * (b + 1), :] = combined[
                PAIR * p : PAIR * (p + 1), b * 128 : (b + 1) * 128
            ]
    wait_pieces = exchange_line(here, pieces2_ref, landed2_ref, act_send, act_recv)
    wait_pieces()
    pair = landed2_ref[...]
    sums = jnp.sum(jnp.sum(pair * pair, axis=0), axis=1, keepdims=True)
    token = lax.broadcasted_iota(jnp.int32, (PAIR * 4, 1), 0) % PAIR
    mean0 = jnp.sum(jnp.where(token == 0, sums, 0.0), axis=0, keepdims=True) * (1.0 / FEATURES)
    mean1 = jnp.sum(jnp.where(token == 1, sums, 0.0), axis=0, keepdims=True) * (1.0 / FEATURES)
    acts = pair * lax.rsqrt(jnp.where(token == 0, mean0, mean1) + epsilon)[None]
    for p in range(LINE):
        for b in range(4):
            at = p * width + b * 128
            acts_ref[:, at : at + 128] = acts[p, PAIR * b : PAIR * (b + 1), :].astype(BF16)

    by_core(c, factor.finish)
    by_core(c, activations.finish)
    for place in (1, 2, 3):
        spread(place).wait_send()

    @pl.when(source)
    def _():
        for i in range(1, NZ):
            lead_z(i).wait_send()

    @pl.when(y == 0)
    def _():
        for i in range(1, NY):
            lead_y(i).wait_send()

    lead_other(c).wait_send()

    @pl.when(layer < DEPTH - 1)
    def _():
        hand_on(following).wait_send()


def forward(tokens, weight, panel, mask):
    width = FEATURES // LINE
    hbm = pl.BlockSpec(memory_space=pl.ANY)
    vmem = pl.BlockSpec(memory_space=pltpu.VMEM)
    dma = pltpu.SemaphoreType.DMA
    return pl.pallas_call(
        forward_kernel,
        out_shape=(
            jax.ShapeDtypeStruct((PAIR, FEATURES), BF16),
            jax.ShapeDtypeStruct((UNITS, LEAD), BF16),
        ),
        in_specs=[hbm] * 4,
        out_specs=(vmem, vmem),
        scratch_shapes=[
            pltpu.VMEM(tokens.shape, BF16),
            pltpu.VMEM(panel.shape, F32),
            pltpu.VMEM(mask.shape, jnp.int32),
            pltpu.VMEM((UNITS, LEAD), BF16),
            pltpu.VMEM((2, LEAD, BLOCK), BF16),
            pltpu.VMEM((LEAD, UNITS), F32),
            pltpu.VMEM((2, LEAD, UNITS), BF16),
            pltpu.VMEM((Z_SLOTS, 2, TOKENS, width), BF16),
            pltpu.VMEM((LINE, UNITS, width), BF16),
            pltpu.VMEM((Z_SLOTS, 2, Y_PLACES, *panel.shape), BF16),
            pltpu.VMEM((TOKENS, UNITS + LEAD), F32),
            pltpu.VMEM((TOKENS, 128), F32),
            pltpu.VMEM((NY, QUARTER, UNITS), BF16),
            pltpu.VMEM((NY, QUARTER, UNITS), BF16),
            pltpu.VMEM((QUARTER, UNITS), BF16),
            pltpu.VMEM((LINE, PAIR * 4, 128), F32),
            pltpu.VMEM((LINE, PAIR * 4, 128), F32),
            pltpu.VMEM((LINE, PAIR * 4, 128), F32),
            pltpu.VMEM((LINE, PAIR * 4, 128), F32),
            dma((LINE + 4,)),
            dma((12,)),
            dma((12,)),
            dma((LINE,)),
            dma((LINE,)),
            dma((LINE,)),
            dma((LINE,)),
            dma((NY,)),
            dma((NY,)),
            dma,
            dma,
            *GATHER_SEMS,
            *GATHER_SEMS,
        ],
        compiler_params=pltpu.CompilerParams(
            collective_id=0, has_side_effects=True, vmem_limit_bytes=60 * 2**20
        ),
        name="forward",
    )(tokens, weight, panel, mask)


def per_device(tokens, up_weight, hess_panel, keep_mask):
    acts, pruned = forward(tokens, up_weight[0], hess_panel[0], keep_mask[0])
    return (acts[None], pruned[None])


def solution(mesh):
    in_specs = (
        P("row", None),
        P("layer", "row", None),
        P("layer", None, "row"),
        P("layer", "row", None),
    )
    out_specs = (P("layer", "row", None), P("layer", "row", None))
    return jax.shard_map(
        per_device, mesh=mesh, in_specs=in_specs, out_specs=out_specs, check_vma=False
    )
```

```python
import functools

import jax
import jax.numpy as jnp
from jax import lax
from jax.experimental import pallas as pl
from jax.experimental.pallas import tpu as pltpu
from jax.sharding import PartitionSpec as P

MESH = pl.DeviceIdType.MESH
TRANSPOSED = (((1,), (1,)), ((), ()))
BF16 = jnp.bfloat16
F32 = jnp.float32

BLOCK = 128
LEAD = 2 * BLOCK
DEPTH = 4
NY = 4
NZ = 8
LINE = 2 * NZ
FEATURES = 8192
UNITS = 512
TOKENS = 128
QUARTER = TOKENS // NY
PAIR = 2
SHARE = LEAD // NY
epsilon = 1e-05

DOWN = 2.0**-32
UP = 2.0**32


def position():
    layer = lax.axis_index("layer")
    row = lax.axis_index("row")
    return layer, row // LINE, (row // 2) % NZ, row % 2


def device(layer, y, z, core):
    return (layer, (y * NZ + z) * 2 + core)


def meet(partners):
    barrier = pltpu.get_barrier_semaphore()
    for partner in partners:
        pl.semaphore_signal(barrier, inc=1, device_id=partner, device_id_type=MESH)
    pl.semaphore_wait(barrier, len(partners))


def remote(src, dst, send_sem, recv_sem, target):
    return pltpu.make_async_remote_copy(
        src_ref=src,
        dst_ref=dst,
        send_sem=send_sem,
        recv_sem=recv_sem,
        device_id=target,
        device_id_type=MESH,
    )


Z_SLOTS = 8
NEAR = slice(0, 5)
FAR = slice(5, 8)


def slot_z(z, k):
    s = 1 - 2 * (z % 2)
    return (z + NZ + [0, -1, 1, -2 * s, 2 * s, -3, 3, 4][k]) % NZ


def number(condition):
    return condition.astype(jnp.int32)


def z_slot(z, target):
    odd = z % 2
    d = (target - z + NZ) % NZ
    fixed = number(d == 7) + 2 * number(d == 1) + 5 * number(d == 5) + 6 * number(d == 3) + 7 * number(d == 4)
    return fixed + (4 - odd) * number(d == 2) + (3 + odd) * number(d == 6)


class Gather:
    def __init__(self, here, view, sems):
        self.layer, self.y, self.z, self.c = here
        self.view = view
        self.send_sems, self.recv_sems = sems
        odd = self.z % 2
        self.on, self.two_on, self.back = 1 - 2 * odd, 2 - 4 * odd, 2 * odd - 1
        self.two = {2: 3 + odd, -2: 4 - odd}
        self.behind_in, self.ahead_in = 2 + odd, 3 - odd
        self.behind_slot, self.behind_out = 5 + odd, 4 + odd
        self.ahead_slot, self.ahead_out = 6 - odd, 5 - odd
        self.sent = {}

    def copy(self, core, src, dst, dy, dz, message):
        src, dst = (self.view(slots, core, part) for slots, part in (src, dst))
        target = device(self.layer, (self.y + dy + NY) % NY, (self.z + dz + NZ) % NZ, core)
        return remote(src, dst, self.send_sems.at[message], self.recv_sems.at[message], target)

    def send(self, core, src, dst, dy, dz, message, name=None):
        self.copy(core, src, dst, dy, dz, message).start()
        self.keep(core, name or message, lambda core: self.copy(core, src, dst, dy, dz, message).wait_send())

    def arrive(self, core, dst, message):
        self.copy(core, dst, dst, 1, 0, message).wait_recv()

    def z_out(self, core, places):
        own = (0, places)
        for dz, message in ((2, 2), (-2, 3)):
            self.send(core, own, (self.two[dz], places), 0, dz, message)
        self.send(core, own, (1, places), 0, 1, 0)
        self.send(core, own, (2, places), 0, -1, 1)

    def z_relay(self, core, places):
        behind, ahead = (3, places), (4, places)
        self.arrive(core, behind, self.behind_in)
        self.send(core, behind, (7, places), 0, self.two_on, 6)
        self.send(core, behind, (self.behind_slot, places), 0, self.on, self.behind_out, "behind")
        self.arrive(core, ahead, self.ahead_in)
        self.send(core, ahead, (self.ahead_slot, places), 0, self.back, self.ahead_out, "ahead")

    def z_in(self, core, places, slots):
        for slot in slots:
            self.arrive(core, (slot, places), {1: 0, 2: 1, 5: 4, 6: 5, 7: 6}[slot])

    def other(self, core, slots, message):
        view = self.view(slots, core, None)
        target = device(self.layer, self.y, self.z, 1 - core)
        return remote(view, view, self.send_sems.at[message], self.recv_sems.at[message], target)

    def to_other(self, core, slots, message):
        self.other(core, slots, message).start()
        self.keep(core, message, lambda core: self.other(core, slots, message).wait_send())

    def from_other(self, slots, message):
        self.other(1 - self.c, slots, message).wait_recv()

    def keep(self, core, name, wait):
        branch = core if isinstance(core, int) else "both"
        self.sent.setdefault(branch, {})[name] = wait

    def finish(self, core):
        for wait in self.sent[core if isinstance(core, int) else "both"].values():
            wait(core)


class TokenGather(Gather):
    def y_out(self, core, slots, message):
        own = (slots, self.y)
        for dy in (2, 1, 3):
            self.send(core, own, own, dy, 0, message + dy - 1)

    def y_in(self, core, slots, message):
        for dy in (1, 3, 2):
            self.arrive(core, (slots, (self.y + NY - dy) % NY), message + dy - 1)

    def part(self, core, i):
        if core == 0:
            if i == 0:
                self.z_out(core, self.y)
                self.y_out(core, 0, 7)
            elif i == 1:
                self.z_relay(core, self.y)
                self.z_in(core, self.y, (1, 2))
                self.y_out(core, slice(1, 5), 10)
            elif i == 2:
                self.z_in(core, self.y, (5, 6, 7))
                self.y_out(core, FAR, 13)
            elif i == 3:
                self.y_in(core, 0, 7)
                self.y_in(core, slice(1, 5), 10)
                self.to_other(core, NEAR, 16)
            else:
                self.y_in(core, FAR, 13)
                self.to_other(core, FAR, 17)
        else:
            if i == 0:
                self.y_out(core, 0, 7)
            elif i == 1:
                self.y_in(core, 0, 7)
                self.z_out(core, None)
            elif i == 2:
                self.z_relay(core, None)
            elif i == 3:
                self.z_in(core, None, (1, 2))
                self.to_other(core, NEAR, 16)
            else:
                self.z_in(core, None, (5, 6, 7))
                self.to_other(core, FAR, 17)


class FactorGather(Gather):
    def __init__(self, here, own_ref, landing, view, sems):
        super().__init__(here, view, sems)
        self.own_ref, self.landing = own_ref, landing

    def rows_to(self, dy):
        to = (self.y + dy) % NY
        return remote(
            self.own_ref.at[pl.ds(to * SHARE, SHARE)],
            self.landing(to),
            self.send_sems.at[6 + dy],
            self.recv_sems.at[6 + dy],
            device(self.layer, to, self.z, self.c),
        )

    def part(self, core, i):
        if i == 0:
            for dy in (2, 1, 3):
                self.rows_to(dy).start()
                self.keep(core, 6 + dy, lambda core, dy=dy: self.rows_to(dy).wait_send())
        elif i == 1:
            for dy in (1, 3, 2):
                self.arrive(core, (0, (self.y + NY - dy) % NY), 6 + dy)
            self.z_out(core, None)
        elif i == 2:
            self.z_relay(core, None)
        elif i == 3:
            self.z_in(core, None, (1, 2))
            self.to_other(core, NEAR, 16)
        else:
            self.z_in(core, None, (5, 6, 7))
            self.to_other(core, FAR, 17)


GATHER_SEMS = [pltpu.SemaphoreType.DMA((18,)), pltpu.SemaphoreType.DMA((18,))]


def by_core(c, part):
    for core in (0, 1):
        pl.when(c == core)(functools.partial(part, core))


SUB = 16


def eliminate(weight_ref, mask_ref, factor_ref, pruned_ref, errors_ref, scaled_ref):
    work = weight_ref[...].astype(F32).T
    first, second = factor_ref[0].astype(F32), factor_ref[1].astype(F32)
    eye = (
        lax.broadcasted_iota(jnp.int32, (BLOCK, BLOCK), 0)
        == lax.broadcasted_iota(jnp.int32, (BLOCK, BLOCK), 1)
    )
    diagonal = jnp.concatenate(
        [
            jnp.sum(jnp.where(eye, first[:BLOCK], 0.0), axis=1, keepdims=True),
            jnp.sum(jnp.where(eye, second[BLOCK:], 0.0), axis=1, keepdims=True),
        ],
        0,
    )
    dropped = 1.0 - mask_ref[...].astype(F32).T
    scaled_ref[...] = dropped * (1.0 / diagonal)
    turned = jnp.concatenate([first.T, second.T], 0)
    turned16 = turned.astype(BF16)
    count = LEAD // SUB
    finished = []
    high, low = [], []
    window = work[: 2 * SUB]
    for g in range(count):
        start = g * SUB
        final = g + 1 == count
        rows = SUB if final else 2 * SUB
        current = window[:rows]
        following = None
        if g + 2 < count:
            following = work[start + 2 * SUB : start + 3 * SUB]
            if g > 0:
                part = turned16[start + 2 * SUB : start + 3 * SUB, :start]
                following = (
                    following
                    - jnp.dot(part, jnp.concatenate(high, 0), preferred_element_type=F32)
                    - jnp.dot(part, jnp.concatenate(low, 0), preferred_element_type=F32)
                )
        local = []
        for o in range(SUB):
            j = start + o
            error = current[o : o + 1] * scaled_ref[j : j + 1, :]
            current = current - turned[start : start + rows, j : j + 1] * error
            local.append(error)
        errors = jnp.concatenate(local, 0)
        errors_high = errors.astype(BF16)
        errors_low = (errors - errors_high.astype(F32)).astype(BF16)
        high.append(errors_high)
        low.append(errors_low)
        finished.append(current[:SUB])
        if not final:
            window = current[SUB:]
            if following is not None:
                part = turned16[start + 2 * SUB : start + 3 * SUB, start : start + SUB]
                following = (
                    following
                    - jnp.dot(part, errors_high, preferred_element_type=F32)
                    - jnp.dot(part, errors_low, preferred_element_type=F32)
                )
                window = jnp.concatenate([window, following], 0)
    pruned_ref[...] = jnp.concatenate(finished, 0).T.astype(BF16)
    errors_ref[0] = jnp.concatenate(high, 0)
    errors_ref[1] = jnp.concatenate(low, 0)


def exchange_line(here, pieces, landed, send_sem, recv_sem):
    layer, y, z, c = here
    me = 2 * z + c
    for i in range(1, LINE):
        peer = (me + i) % LINE
        remote(
            pieces.at[peer], landed.at[me], send_sem, recv_sem, device(layer, y, peer // 2, peer % 2)
        ).start()
    landed[me] = pieces[me]


def exchange_wait(here, pieces, landed, send_sem, recv_sem):
    layer, y, z, c = here
    others = pl.ds(0, LINE - 1)
    every = remote(pieces.at[others], landed.at[others], send_sem, recv_sem, device(layer, y, z, 1 - c))
    every.wait_recv()
    every.wait_send()


def silu(v):
    return v / (1.0 + jnp.exp(-v))


def forward_kernel(
    tokens_hbm,
    weight_ref,
    panel_hbm,
    mask_hbm,
    acts_ref,
    pruned_ref,
    tokens_ref,
    panel_ref,
    mask_ref,
    leading_ref,
    lead_ref,
    scaled_ref,
    errors_ref,
    x_ref,
    w_ref,
    u_ref,
    total_ref,
    inputs_ref,
    every_input_ref,
    own_ref,
    squares_ref,
    scale_ref,
    out_ref,
    spread_ref,
    hand_ref,
    pieces_ref,
    landed_ref,
    pieces2_ref,
    landed2_ref,
    load_sems,
    lead_send,
    lead_recv,
    token_send,
    token_recv,
    act_send,
    act_recv,
    share_send,
    share_recv,
    inputs_send,
    inputs_recv,
    spread_send,
    spread_recv,
    hand_send,
    hand_recv,
    *sems,
):
    here = position()
    layer, y, z, c = here
    me = 2 * z + c
    width = FEATURES // LINE

    loads = [
        pltpu.make_async_copy(panel_hbm, panel_ref, load_sems.at[0]),
        pltpu.make_async_copy(tokens_hbm, tokens_ref, load_sems.at[1]),
        pltpu.make_async_copy(mask_hbm, mask_ref, load_sems.at[2]),
        pltpu.make_async_copy(weight_ref.at[:, pl.ds(0, LEAD)], leading_ref, load_sems.at[3]),
        pltpu.make_async_copy(
            weight_ref.at[:, pl.ds(LEAD, width - LEAD)],
            w_ref.at[0, :, pl.ds(LEAD, width - LEAD)],
            load_sems.at[4],
        ),
    ]
    for k in range(1, LINE):
        loads.append(
            pltpu.make_async_copy(
                weight_ref.at[:, pl.ds(k * width, width)], w_ref.at[k], load_sems.at[4 + k]
            )
        )
    for load in loads:
        load.start()

    partners = [device(layer, y, ((me + i) % LINE) // 2, (me + i) % 2) for i in range(1, LINE)]
    partners += [device(layer, (y + i) % NY, z, c) for i in range(1, NY)]
    partners += [device((layer + i) % DEPTH, y, z, c) for i in (1, DEPTH - 1)]
    meet(partners)

    def x_view(slots, core, part):
        rows = pl.ds(0, TOKENS) if part is None else pl.ds(pl.multiple_of(part * QUARTER, QUARTER), QUARTER)
        return x_ref.at[slots, core, rows, :]

    def u_view(slots, core, part):
        return u_ref.at[y, slots, core] if part is None else u_ref.at[y, slots, core, part]

    activations = TokenGather(here, x_view, sems[:2])
    factor = FactorGather(here, own_ref, lambda to: u_ref.at[to, 0, c, y], u_view, sems[2:])

    loads[0].wait()
    mine = panel_ref[...].astype(BF16)
    source = (y == 0) & (z == 0)
    my_rows = pl.ds(pl.multiple_of(y * QUARTER, QUARTER), QUARTER)
    own_ref[...] = jnp.where(source, 0.0, panel_ref[...]).astype(BF16)
    u_ref[y, 0, c, y] = own_ref[pl.ds(pl.multiple_of(y * SHARE, SHARE), SHARE), :]

    def lead_copy(core, target, message):
        return remote(lead_ref.at[core], lead_ref.at[core], lead_send.at[message], lead_recv.at[message], target)

    def lead_z(i):
        return lead_copy(c, device(layer, 0, i, c), i)

    def lead_y(i):
        return lead_copy(c, device(layer, i, z, c), 7 + i)

    def lead_other(core):
        return lead_copy(core, device(layer, y, z, 1 - c), 11)

    @pl.when(source)
    def _():
        lead_ref[c] = mine
        for i in (4, 3, 5, 2, 6, 1, 7):
            lead_z(i).start()

    @pl.when(layer == 0)
    def _():
        loads[1].wait()
        tokens = tokens_ref[...].astype(F32)
        for p in range(LINE):
            for b in range(4):
                at = p * width + b * 128
                pieces_ref[p, PAIR * b : PAIR * (b + 1), :] = tokens[:, at : at + 128]
        exchange_line(here, pieces_ref, landed_ref, token_send, token_recv)

    factor.part(c, 0)

    @pl.when((y == 0) & (z > 0))
    def _():
        lead_copy(c, device(layer, 0, 0, c), z).wait_recv()

    @pl.when(y == 0)
    def _():
        for i in (2, 1, 3):
            lead_y(i).start()

    @pl.when(layer == 0)
    def _():
        exchange_wait(here, pieces_ref, landed_ref, token_send, token_recv)
        for p in range(LINE):
            for b in range(4):
                total_ref[PAIR * p : PAIR * (p + 1), b * 128 : (b + 1) * 128] = landed_ref[
                    p, PAIR * b : PAIR * (b + 1), :
                ]
        x_ref[0, c, my_rows, :] = total_ref[:QUARTER, :].astype(BF16)

    def gather_parts(*parts):
        for i in parts:
            pl.when(layer == 0)(lambda: by_core(c, lambda core: activations.part(core, i)))
            if i:
                factor.part(c, i)

    gather_parts(0, 1, 2)

    @pl.when(y > 0)
    def _():
        lead_copy(c, device(layer, 0, z, c), 7 + y).wait_recv()

    lead_other(c).start()
    gather_parts(3)

    def share_to(dy):
        mine = u_ref.at[y, :, c]
        return remote(mine, mine, share_send.at[dy], share_recv.at[dy], device(layer, (y + dy) % NY, z, c))

    def share_from(dy, core):
        theirs = u_ref.at[(y + NY - dy) % NY, :, core]
        return remote(
            theirs, theirs, share_send.at[3 + dy], share_recv.at[3 + dy], device(layer, y, z, 1 - c)
        )

    @pl.when(layer > 0)
    def _():
        factor.part(c, 4)
        factor.from_other(NEAR, 16)
        factor.from_other(FAR, 17)
        for dy in (2, 1, 3):
            share_to(dy).start()

    for load in loads[2:4]:
        load.wait()
    lead_other(1 - c).wait_recv()
    eliminate(leading_ref, mask_ref, lead_ref, pruned_ref, errors_ref, scaled_ref)

    @pl.when(layer > 0)
    def _():
        loads[1].wait()

    for load in loads[4:]:
        load.wait()
    w_ref[0, :, :LEAD] = pruned_ref[...]
    total_ref[...] = jnp.zeros_like(total_ref)
    inputs_ref[y] = jnp.zeros_like(inputs_ref[y])
    every_input_ref[...] = jnp.zeros_like(every_input_ref)
    squares_ref[...] = jnp.zeros_like(squares_ref)

    @pl.when(layer == 0)
    def _():
        factor.part(c, 4)
        factor.from_other(NEAR, 16)
        factor.from_other(FAR, 17)

    def hand_on(target):
        return remote(hand_ref, x_ref.at[0, c, my_rows, :], hand_send, hand_recv, target)

    def inputs_to(dy):
        mine = inputs_ref.at[y]
        return remote(mine, mine, inputs_send.at[dy], inputs_recv.at[dy], device(layer, (y + dy) % NY, z, c))

    @pl.when(layer > 0)
    def _():
        for dy in (1, 3, 2):
            theirs = u_ref.at[(y + NY - dy) % NY, :, c]
            target = device(layer, (y + dy) % NY, z, c)
            remote(theirs, theirs, share_send.at[dy], share_recv.at[dy], target).wait_recv()
            share_from(dy, c).start()
        for dy in (1, 3, 2):
            share_from(dy, 1 - c).wait_recv()
            share_from(dy, c).wait_send()
            share_to(dy).wait_send()
        hand_on(device((layer + DEPTH - 1) % DEPTH, y, z, c)).wait_recv()

        def near_activations(core):
            for i in range(4):
                activations.part(core, i)

        by_core(c, near_activations)

    def add(old, new):
        return new if old is None else old + new

    def multiply(slots, core, shares=(), weights=True, turned=False):
        products, entries, squares = None, None, None
        for slot in slots:
            k = 2 * slot_z(z, slot) + core
            x = x_ref[slot, core]
            if weights:
                products = add(
                    products, lax.dot_general(x, w_ref[k], TRANSPOSED, preferred_element_type=F32)
                )
            if shares:
                sides = [z_slot(z, 2 * (k % 4)), z_slot(z, 2 * (k % 4) + 1)]
                columns = [
                    jnp.concatenate([u_ref[share, sides[j // 2], j % 2, k // 4] for j in range(4)], 1)
                    for share in shares
                ]
                columns = columns[0] if len(columns) == 1 else jnp.concatenate(columns, 0)
                left, right = (columns, x) if turned else (x, columns)
                entries = add(entries, lax.dot_general(left, right, TRANSPOSED, preferred_element_type=F32))
                wide = x.astype(F32)
                wide = wide * wide
                squares = add(
                    squares, wide[:, :128] + wide[:, 128:256] + wide[:, 256:384] + wide[:, 384:]
                )
        if weights:
            total_ref[...] += products
        if shares:
            if turned:
                inputs_ref[y] += entries
            else:
                every_input_ref[...] += entries
            squares_ref[...] += squares

    def both(numbers, message, **what):
        def one(i, carry):
            if message is not None:

                @pl.when(i == 1)
                def _():
                    activations.from_other(slice(numbers.start, numbers.stop), message)

            multiply(numbers, c + i * (1 - 2 * c), **what)
            return carry

        lax.fori_loop(0, 2, one, 0)

    near, far = range(NEAR.start, NEAR.stop), range(FAR.start, FAR.stop)

    @pl.when(layer == 0)
    def _():
        both(near, 16, shares=[y], turned=True)
        by_core(c, lambda core: activations.part(core, 4))
        both(far, 17, shares=[y], weights=False, turned=True)
        for dy in (2, 1, 3):
            inputs_to(dy).start()
        both(far, None)
        for dy in (1, 3, 2):
            theirs = inputs_ref.at[(y + NY - dy) % NY]
            target = device(layer, (y + dy) % NY, z, c)
            remote(theirs, theirs, inputs_send.at[dy], inputs_recv.at[dy], target).wait_recv()
        for dy in (1, 3, 2):
            inputs_to(dy).wait_send()
        every_input_ref[...] = jnp.concatenate([inputs_ref[i] for i in range(NY)], 0).T

    @pl.when(layer > 0)
    def _():
        both(near, 16, shares=list(range(NY)))
        by_core(c, lambda core: activations.part(core, 4))
        both(far, 17, shares=list(range(NY)))

    moment = jnp.sum(squares_ref[...], axis=1, keepdims=True) * (UP * UP / FEATURES)
    scale = jnp.where(layer == 0, 1.0, lax.rsqrt(moment + epsilon) * UP)
    inputs = every_input_ref[...]
    inputs_high = inputs.astype(BF16)
    inputs_low = (inputs - inputs_high.astype(F32)).astype(BF16)
    correction = (
        jnp.dot(inputs_high, errors_ref[0], preferred_element_type=F32)
        + jnp.dot(inputs_low, errors_ref[0], preferred_element_type=F32)
        + jnp.dot(inputs_high, errors_ref[1], preferred_element_type=F32)
    )
    output = ((total_ref[...] - correction) * (scale * FEATURES**-0.5)).astype(BF16)
    for q in range(NY):
        out_ref[q] = output[q * QUARTER : (q + 1) * QUARTER]
    scale_ref[...] = jnp.broadcast_to(scale, scale_ref.shape)

    def spread(dy):
        q = (y + dy) % NY
        return remote(
            out_ref.at[q], spread_ref.at[dy], spread_send.at[dy], spread_recv.at[dy], device(layer, q, z, c)
        )

    for dy in (2, 1, 3):
        spread(dy).start()
    residual = x_ref[0, c, my_rows, :].astype(F32) * scale_ref[my_rows, :1]
    combined = residual + silu(out_ref[y].astype(F32))
    for dy in (1, 3, 2):
        spread(dy).wait_recv()
        combined = combined + silu(spread_ref[dy].astype(F32))
    following = device((layer + 1) % DEPTH, y, z, c)

    @pl.when(layer < DEPTH - 1)
    def _():
        hand_ref[...] = (combined * DOWN).astype(BF16)
        hand_on(following).start()

    for p in range(LINE):
        for b in range(4):
            pieces2_ref[p, PAIR * b : PAIR * (b + 1), :] = combined[
                PAIR * p : PAIR * (p + 1), b * 128 : (b + 1) * 128
            ]
    exchange_line(here, pieces2_ref, landed2_ref, act_send, act_recv)
    factor.finish(c)
    by_core(c, activations.finish)
    for dy in (1, 2, 3):
        spread(dy).wait_send()

    @pl.when(source)
    def _():
        for i in range(1, NZ):
            lead_z(i).wait_send()

    @pl.when(y == 0)
    def _():
        for i in range(1, NY):
            lead_y(i).wait_send()

    lead_other(c).wait_send()

    @pl.when(layer < DEPTH - 1)
    def _():
        hand_on(following).wait_send()
    exchange_wait(here, pieces2_ref, landed2_ref, act_send, act_recv)
    pair = landed2_ref[...]
    sums = jnp.sum(jnp.sum(pair * pair, axis=0), axis=1, keepdims=True)
    token = lax.broadcasted_iota(jnp.int32, (PAIR * 4, 1), 0) % PAIR
    mean0 = jnp.sum(jnp.where(token == 0, sums, 0.0), axis=0, keepdims=True) * (1.0 / FEATURES)
    mean1 = jnp.sum(jnp.where(token == 1, sums, 0.0), axis=0, keepdims=True) * (1.0 / FEATURES)
    acts = pair * lax.rsqrt(jnp.where(token == 0, mean0, mean1) + epsilon)[None]
    for p in range(LINE):
        for b in range(4):
            at = p * width + b * 128
            acts_ref[:, at : at + 128] = acts[p, PAIR * b : PAIR * (b + 1), :].astype(BF16)


def forward(tokens, weight, panel, mask):
    width = FEATURES // LINE
    hbm = pl.BlockSpec(memory_space=pl.ANY)
    vmem = pl.BlockSpec(memory_space=pltpu.VMEM)
    dma = pltpu.SemaphoreType.DMA
    return pl.pallas_call(
        forward_kernel,
        out_shape=(
            jax.ShapeDtypeStruct((PAIR, FEATURES), BF16),
            jax.ShapeDtypeStruct((UNITS, LEAD), BF16),
        ),
        in_specs=[hbm] * 4,
        out_specs=(vmem, vmem),
        scratch_shapes=[
            pltpu.VMEM(tokens.shape, BF16),
            pltpu.VMEM(panel.shape, F32),
            pltpu.VMEM(mask.shape, jnp.int32),
            pltpu.VMEM((UNITS, LEAD), BF16),
            pltpu.VMEM((2, LEAD, BLOCK), BF16),
            pltpu.VMEM((LEAD, UNITS), F32),
            pltpu.VMEM((2, LEAD, UNITS), BF16),
            pltpu.VMEM((Z_SLOTS, 2, TOKENS, width), BF16),
            pltpu.VMEM((LINE, UNITS, width), BF16),
            pltpu.VMEM((NY, Z_SLOTS, 2, NY, SHARE, 128), BF16),
            pltpu.VMEM((TOKENS, UNITS), F32),
            pltpu.VMEM((NY, SHARE, TOKENS), F32),
            pltpu.VMEM((TOKENS, LEAD), F32),
            pltpu.VMEM(panel.shape, BF16),
            pltpu.VMEM((TOKENS, 128), F32),
            pltpu.VMEM((TOKENS, 128), F32),
            pltpu.VMEM((NY, QUARTER, UNITS), BF16),
            pltpu.VMEM((NY, QUARTER, UNITS), BF16),
            pltpu.VMEM((QUARTER, UNITS), BF16),
            pltpu.VMEM((LINE, PAIR * 4, 128), F32),
            pltpu.VMEM((LINE, PAIR * 4, 128), F32),
            pltpu.VMEM((LINE, PAIR * 4, 128), F32),
            pltpu.VMEM((LINE, PAIR * 4, 128), F32),
            dma((LINE + 4,)),
            dma((12,)),
            dma((12,)),
            dma,
            dma,
            dma,
            dma,
            dma((7,)),
            dma((7,)),
            dma((NY,)),
            dma((NY,)),
            dma((NY,)),
            dma((NY,)),
            dma,
            dma,
            *GATHER_SEMS,
            *GATHER_SEMS,
        ],
        compiler_params=pltpu.CompilerParams(
            collective_id=0, has_side_effects=True, vmem_limit_bytes=60 * 2**20
        ),
        name="forward",
    )(tokens, weight, panel, mask)


def hand_out_kernel(acts_in, pruned_in, acts_out, pruned_out):
    acts_out[...] = acts_in[...]
    pruned_out[...] = pruned_in[...]


def hand_out(acts, pruned):
    vmem = pl.BlockSpec(memory_space=pltpu.VMEM)
    return pl.pallas_call(
        hand_out_kernel,
        out_shape=(
            jax.ShapeDtypeStruct(acts.shape, acts.dtype),
            jax.ShapeDtypeStruct(pruned.shape, pruned.dtype),
        ),
        in_specs=[vmem, vmem],
        out_specs=(vmem, vmem),
        name="hand_out",
    )(acts, pruned)


def per_device(tokens, up_weight, hess_panel, keep_mask):
    acts, pruned = hand_out(*forward(tokens, up_weight[0], hess_panel[0], keep_mask[0]))
    return (acts[None], pruned[None])


def solution(mesh):
    in_specs = (
        P("row", None),
        P("layer", "row", None),
        P("layer", None, "row"),
        P("layer", "row", None),
    )
    out_specs = (P("layer", "row", None), P("layer", "row", None))
    return jax.shard_map(
        per_device, mesh=mesh, in_specs=in_specs, out_specs=out_specs, check_vma=False
    )
```

```python
import functools

import jax
import jax.numpy as jnp
from jax import lax
from jax.experimental import pallas as pl
from jax.experimental.pallas import tpu as pltpu
from jax.sharding import PartitionSpec as P

MESH = pl.DeviceIdType.MESH
TRANSPOSED = (((1,), (1,)), ((), ()))
BF16 = jnp.bfloat16
F32 = jnp.float32

BLOCK = 128
LEAD = 2 * BLOCK
DEPTH = 4
NY = 4
NZ = 8
LINE = 2 * NZ
FEATURES = 8192
UNITS = 512
TOKENS = 128
QUARTER = TOKENS // NY
PAIR = 2
SHARE = LEAD // NY
epsilon = 1e-05

DOWN = 2.0**-32
UP = 2.0**32


def position():
    layer = lax.axis_index("layer")
    row = lax.axis_index("row")
    return layer, row // LINE, (row // 2) % NZ, row % 2


def device(layer, y, z, core):
    return (layer, (y * NZ + z) * 2 + core)


def meet(partners):
    barrier = pltpu.get_barrier_semaphore()
    for partner in partners:
        pl.semaphore_signal(barrier, inc=1, device_id=partner, device_id_type=MESH)
    pl.semaphore_wait(barrier, len(partners))


def remote(src, dst, send_sem, recv_sem, target):
    return pltpu.make_async_remote_copy(
        src_ref=src,
        dst_ref=dst,
        send_sem=send_sem,
        recv_sem=recv_sem,
        device_id=target,
        device_id_type=MESH,
    )


Z_SLOTS = 8
NEAR = slice(0, 5)
FAR = slice(5, 8)


def slot_z(z, k):
    s = 1 - 2 * (z % 2)
    return (z + NZ + [0, -1, 1, -2 * s, 2 * s, -3, 3, 4][k]) % NZ


def number(condition):
    return condition.astype(jnp.int32)


def z_slot(z, target):
    odd = z % 2
    d = (target - z + NZ) % NZ
    fixed = number(d == 7) + 2 * number(d == 1) + 5 * number(d == 5) + 6 * number(d == 3) + 7 * number(d == 4)
    return fixed + (4 - odd) * number(d == 2) + (3 + odd) * number(d == 6)


class Gather:
    def __init__(self, here, view, sems):
        self.layer, self.y, self.z, self.c = here
        self.view = view
        self.send_sems, self.recv_sems = sems
        odd = self.z % 2
        self.on, self.two_on, self.back = 1 - 2 * odd, 2 - 4 * odd, 2 * odd - 1
        self.two = {2: 3 + odd, -2: 4 - odd}
        self.behind_in, self.ahead_in = 2 + odd, 3 - odd
        self.behind_slot, self.behind_out = 5 + odd, 4 + odd
        self.ahead_slot, self.ahead_out = 6 - odd, 5 - odd
        self.sent = {}

    def copy(self, core, src, dst, dy, dz, message):
        src, dst = (self.view(slots, core, part) for slots, part in (src, dst))
        target = device(self.layer, (self.y + dy + NY) % NY, (self.z + dz + NZ) % NZ, core)
        return remote(src, dst, self.send_sems.at[message], self.recv_sems.at[message], target)

    def send(self, core, src, dst, dy, dz, message, name=None):
        self.copy(core, src, dst, dy, dz, message).start()
        self.keep(core, name or message, lambda core: self.copy(core, src, dst, dy, dz, message).wait_send())

    def arrive(self, core, dst, message):
        self.copy(core, dst, dst, 1, 0, message).wait_recv()

    def z_out(self, core, places):
        own = (0, places)
        for dz, message in ((2, 2), (-2, 3)):
            self.send(core, own, (self.two[dz], places), 0, dz, message)
        self.send(core, own, (1, places), 0, 1, 0)
        self.send(core, own, (2, places), 0, -1, 1)

    def z_relay(self, core, places):
        behind, ahead = (3, places), (4, places)
        self.arrive(core, behind, self.behind_in)
        self.send(core, behind, (7, places), 0, self.two_on, 6)
        self.send(core, behind, (self.behind_slot, places), 0, self.on, self.behind_out, "behind")
        self.arrive(core, ahead, self.ahead_in)
        self.send(core, ahead, (self.ahead_slot, places), 0, self.back, self.ahead_out, "ahead")

    def z_in(self, core, places, slots):
        for slot in slots:
            self.arrive(core, (slot, places), {1: 0, 2: 1, 5: 4, 6: 5, 7: 6}[slot])

    def other(self, core, slots, message):
        view = self.view(slots, core, None)
        target = device(self.layer, self.y, self.z, 1 - core)
        return remote(view, view, self.send_sems.at[message], self.recv_sems.at[message], target)

    def to_other(self, core, slots, message):
        self.other(core, slots, message).start()
        self.keep(core, message, lambda core: self.other(core, slots, message).wait_send())

    def from_other(self, slots, message):
        self.other(1 - self.c, slots, message).wait_recv()

    def keep(self, core, name, wait):
        branch = core if isinstance(core, int) else "both"
        self.sent.setdefault(branch, {})[name] = wait

    def finish(self, core):
        for wait in self.sent[core if isinstance(core, int) else "both"].values():
            wait(core)


class TokenGather(Gather):
    def y_out(self, core, slots, message):
        own = (slots, self.y)
        for dy in (2, 1, 3):
            self.send(core, own, own, dy, 0, message + dy - 1)

    def y_in(self, core, slots, message):
        for dy in (1, 3, 2):
            self.arrive(core, (slots, (self.y + NY - dy) % NY), message + dy - 1)

    def part(self, core, i):
        if core == 0:
            if i == 0:
                self.z_out(core, self.y)
                self.y_out(core, 0, 7)
            elif i == 1:
                self.z_relay(core, self.y)
                self.z_in(core, self.y, (1, 2))
                self.y_out(core, slice(1, 5), 10)
            elif i == 2:
                self.z_in(core, self.y, (5, 6, 7))
                self.y_out(core, FAR, 13)
            elif i == 3:
                self.y_in(core, 0, 7)
                self.y_in(core, slice(1, 5), 10)
                self.to_other(core, NEAR, 16)
            else:
                self.y_in(core, FAR, 13)
                self.to_other(core, FAR, 17)
        else:
            if i == 0:
                self.y_out(core, 0, 7)
            elif i == 1:
                self.y_in(core, 0, 7)
                self.z_out(core, None)
            elif i == 2:
                self.z_relay(core, None)
            elif i == 3:
                self.z_in(core, None, (1, 2))
                self.to_other(core, NEAR, 16)
            else:
                self.z_in(core, None, (5, 6, 7))
                self.to_other(core, FAR, 17)


class FactorGather(Gather):
    def __init__(self, here, own_ref, landing, view, sems):
        super().__init__(here, view, sems)
        self.own_ref, self.landing = own_ref, landing

    def rows_to(self, dy):
        to = (self.y + dy) % NY
        return remote(
            self.own_ref.at[pl.ds(to * SHARE, SHARE)],
            self.landing(to),
            self.send_sems.at[6 + dy],
            self.recv_sems.at[6 + dy],
            device(self.layer, to, self.z, self.c),
        )

    def part(self, core, i):
        if i == 0:
            for dy in (2, 1, 3):
                self.rows_to(dy).start()
                self.keep(core, 6 + dy, lambda core, dy=dy: self.rows_to(dy).wait_send())
        elif i == 1:
            for dy in (1, 3, 2):
                self.arrive(core, (0, (self.y + NY - dy) % NY), 6 + dy)
            self.z_out(core, None)
        elif i == 2:
            self.z_relay(core, None)
        elif i == 3:
            self.z_in(core, None, (1, 2))
            self.to_other(core, NEAR, 16)
        else:
            self.z_in(core, None, (5, 6, 7))
            self.to_other(core, FAR, 17)


GATHER_SEMS = [pltpu.SemaphoreType.DMA((18,)), pltpu.SemaphoreType.DMA((18,))]


def by_core(c, part):
    for core in (0, 1):
        pl.when(c == core)(functools.partial(part, core))


SUB = 16


def eliminate(weight_ref, mask_ref, factor_ref, pruned_ref, errors_ref, scaled_ref):
    work = weight_ref[...].astype(F32).T
    first, second = factor_ref[0].astype(F32), factor_ref[1].astype(F32)
    eye = (
        lax.broadcasted_iota(jnp.int32, (BLOCK, BLOCK), 0)
        == lax.broadcasted_iota(jnp.int32, (BLOCK, BLOCK), 1)
    )
    diagonal = jnp.concatenate(
        [
            jnp.sum(jnp.where(eye, first[:BLOCK], 0.0), axis=1, keepdims=True),
            jnp.sum(jnp.where(eye, second[BLOCK:], 0.0), axis=1, keepdims=True),
        ],
        0,
    )
    dropped = 1.0 - mask_ref[...].astype(F32).T
    scaled_ref[...] = dropped * (1.0 / diagonal)
    turned = jnp.concatenate([first.T, second.T], 0)
    turned16 = turned.astype(BF16)
    count = LEAD // SUB
    finished = []
    high, low = [], []
    window = work[: 2 * SUB]
    for g in range(count):
        start = g * SUB
        final = g + 1 == count
        rows = SUB if final else 2 * SUB
        current = window[:rows]
        following = None
        if g + 2 < count:
            following = work[start + 2 * SUB : start + 3 * SUB]
            if g > 0:
                part = turned16[start + 2 * SUB : start + 3 * SUB, :start]
                following = (
                    following
                    - jnp.dot(part, jnp.concatenate(high, 0), preferred_element_type=F32)
                    - jnp.dot(part, jnp.concatenate(low, 0), preferred_element_type=F32)
                )
        local = []
        for o in range(SUB):
            j = start + o
            error = current[o : o + 1] * scaled_ref[j : j + 1, :]
            current = current - turned[start : start + rows, j : j + 1] * error
            local.append(error)
        errors = jnp.concatenate(local, 0)
        errors_high = errors.astype(BF16)
        errors_low = (errors - errors_high.astype(F32)).astype(BF16)
        high.append(errors_high)
        low.append(errors_low)
        finished.append(current[:SUB])
        if not final:
            window = current[SUB:]
            if following is not None:
                part = turned16[start + 2 * SUB : start + 3 * SUB, start : start + SUB]
                following = (
                    following
                    - jnp.dot(part, errors_high, preferred_element_type=F32)
                    - jnp.dot(part, errors_low, preferred_element_type=F32)
                )
                window = jnp.concatenate([window, following], 0)
    pruned_ref[...] = jnp.concatenate(finished, 0).T.astype(BF16)
    errors_ref[0] = jnp.concatenate(high, 0)
    errors_ref[1] = jnp.concatenate(low, 0)


def exchange_line(here, pieces, landed, send_sem, recv_sem):
    layer, y, z, c = here
    me = 2 * z + c
    for i in range(1, LINE):
        peer = (me + i) % LINE
        remote(
            pieces.at[peer], landed.at[me], send_sem, recv_sem, device(layer, y, peer // 2, peer % 2)
        ).start()
    landed[me] = pieces[me]


def exchange_wait(here, pieces, landed, send_sem, recv_sem):
    layer, y, z, c = here
    others = pl.ds(0, LINE - 1)
    every = remote(pieces.at[others], landed.at[others], send_sem, recv_sem, device(layer, y, z, 1 - c))
    every.wait_recv()
    every.wait_send()


def silu(v):
    return v / (1.0 + jnp.exp(-v))


def forward_kernel(
    tokens_hbm,
    weight_ref,
    panel_hbm,
    mask_hbm,
    acts_ref,
    pruned_ref,
    tokens_ref,
    panel_ref,
    mask_ref,
    leading_ref,
    lead_ref,
    scaled_ref,
    errors_ref,
    x_ref,
    w_ref,
    u_ref,
    total_ref,
    inputs_ref,
    every_input_ref,
    own_ref,
    squares_ref,
    scale_ref,
    out_ref,
    spread_ref,
    hand_ref,
    pieces_ref,
    landed_ref,
    pieces2_ref,
    landed2_ref,
    load_sems,
    lead_send,
    lead_recv,
    token_send,
    token_recv,
    act_send,
    act_recv,
    share_send,
    share_recv,
    inputs_send,
    inputs_recv,
    spread_send,
    spread_recv,
    hand_send,
    hand_recv,
    *sems,
):
    here = position()
    layer, y, z, c = here
    me = 2 * z + c
    width = FEATURES // LINE

    loads = [
        pltpu.make_async_copy(panel_hbm, panel_ref, load_sems.at[0]),
        pltpu.make_async_copy(tokens_hbm, tokens_ref, load_sems.at[1]),
        pltpu.make_async_copy(mask_hbm, mask_ref, load_sems.at[2]),
        pltpu.make_async_copy(weight_ref.at[:, pl.ds(0, LEAD)], leading_ref, load_sems.at[3]),
        pltpu.make_async_copy(
            weight_ref.at[:, pl.ds(LEAD, width - LEAD)],
            w_ref.at[0, :, pl.ds(LEAD, width - LEAD)],
            load_sems.at[4],
        ),
    ]
    for k in range(1, LINE):
        loads.append(
            pltpu.make_async_copy(
                weight_ref.at[:, pl.ds(k * width, width)], w_ref.at[k], load_sems.at[4 + k]
            )
        )
    for load in loads:
        load.start()

    partners = [device(layer, y, ((me + i) % LINE) // 2, (me + i) % 2) for i in range(1, LINE)]
    partners += [device(layer, (y + i) % NY, z, c) for i in range(1, NY)]
    partners += [device((layer + i) % DEPTH, y, z, c) for i in (1, DEPTH - 1)]
    meet(partners)

    def x_view(slots, core, part):
        rows = pl.ds(0, TOKENS) if part is None else pl.ds(pl.multiple_of(part * QUARTER, QUARTER), QUARTER)
        return x_ref.at[slots, core, rows, :]

    def u_view(slots, core, part):
        return u_ref.at[y, slots, core] if part is None else u_ref.at[y, slots, core, part]

    activations = TokenGather(here, x_view, sems[:2])
    factor = FactorGather(here, own_ref, lambda to: u_ref.at[to, 0, c, y], u_view, sems[2:])

    loads[0].wait()
    mine = panel_ref[...].astype(BF16)
    source = (y == 0) & (z == 0)
    my_rows = pl.ds(pl.multiple_of(y * QUARTER, QUARTER), QUARTER)
    own_ref[...] = jnp.where(source, 0.0, panel_ref[...]).astype(BF16)
    u_ref[y, 0, c, y] = own_ref[pl.ds(pl.multiple_of(y * SHARE, SHARE), SHARE), :]

    def lead_copy(core, target, message):
        return remote(lead_ref.at[core], lead_ref.at[core], lead_send.at[message], lead_recv.at[message], target)

    def lead_z(i):
        return lead_copy(c, device(layer, 0, i, c), i)

    def lead_y(i):
        return lead_copy(c, device(layer, i, z, c), 7 + i)

    def lead_other(core):
        return lead_copy(core, device(layer, y, z, 1 - c), 11)

    @pl.when(source)
    def _():
        lead_ref[c] = mine
        for i in (4, 3, 5, 2, 6, 1, 7):
            lead_z(i).start()

    @pl.when(layer == 0)
    def _():
        loads[1].wait()
        tokens = tokens_ref[...].astype(F32)
        for p in range(LINE):
            for b in range(4):
                at = p * width + b * 128
                pieces_ref[p, PAIR * b : PAIR * (b + 1), :] = tokens[:, at : at + 128]
        exchange_line(here, pieces_ref, landed_ref, token_send, token_recv)

    factor.part(c, 0)

    @pl.when((y == 0) & (z > 0))
    def _():
        lead_copy(c, device(layer, 0, 0, c), z).wait_recv()

    @pl.when(y == 0)
    def _():
        for i in (2, 1, 3):
            lead_y(i).start()

    @pl.when(layer == 0)
    def _():
        exchange_wait(here, pieces_ref, landed_ref, token_send, token_recv)
        for p in range(LINE):
            for b in range(4):
                total_ref[PAIR * p : PAIR * (p + 1), b * 128 : (b + 1) * 128] = landed_ref[
                    p, PAIR * b : PAIR * (b + 1), :
                ]
        x_ref[0, c, my_rows, :] = total_ref[:QUARTER, :].astype(BF16)

    def gather_parts(*parts):
        for i in parts:
            pl.when(layer == 0)(lambda: by_core(c, lambda core: activations.part(core, i)))
            if i:
                factor.part(c, i)

    gather_parts(0, 1, 2)

    @pl.when(y > 0)
    def _():
        lead_copy(c, device(layer, 0, z, c), 7 + y).wait_recv()

    lead_other(c).start()
    gather_parts(3)

    def share_to(dy):
        mine = u_ref.at[y, :, c]
        return remote(mine, mine, share_send.at[dy], share_recv.at[dy], device(layer, (y + dy) % NY, z, c))

    def share_from(dy, core):
        theirs = u_ref.at[(y + NY - dy) % NY, :, core]
        return remote(
            theirs, theirs, share_send.at[3 + dy], share_recv.at[3 + dy], device(layer, y, z, 1 - c)
        )

    @pl.when(layer > 0)
    def _():
        factor.part(c, 4)
        factor.from_other(NEAR, 16)
        factor.from_other(FAR, 17)
        for dy in (2, 1, 3):
            share_to(dy).start()

    for load in loads[2:4]:
        load.wait()
    lead_other(1 - c).wait_recv()
    eliminate(leading_ref, mask_ref, lead_ref, pruned_ref, errors_ref, scaled_ref)

    @pl.when(layer > 0)
    def _():
        loads[1].wait()

    for load in loads[4:]:
        load.wait()
    w_ref[0, :, :LEAD] = pruned_ref[...]
    total_ref[...] = jnp.zeros_like(total_ref)
    inputs_ref[y] = jnp.zeros_like(inputs_ref[y])
    every_input_ref[...] = jnp.zeros_like(every_input_ref)
    squares_ref[...] = jnp.zeros_like(squares_ref)

    @pl.when(layer == 0)
    def _():
        factor.part(c, 4)
        factor.from_other(NEAR, 16)
        factor.from_other(FAR, 17)

    def hand_on(target):
        return remote(hand_ref, x_ref.at[0, c, my_rows, :], hand_send, hand_recv, target)

    def inputs_to(dy):
        mine = inputs_ref.at[y]
        return remote(mine, mine, inputs_send.at[dy], inputs_recv.at[dy], device(layer, (y + dy) % NY, z, c))

    @pl.when(layer > 0)
    def _():
        for dy in (1, 3, 2):
            theirs = u_ref.at[(y + NY - dy) % NY, :, c]
            target = device(layer, (y + dy) % NY, z, c)
            remote(theirs, theirs, share_send.at[dy], share_recv.at[dy], target).wait_recv()
            share_from(dy, c).start()
        for dy in (1, 3, 2):
            share_from(dy, 1 - c).wait_recv()
            share_from(dy, c).wait_send()
            share_to(dy).wait_send()
        hand_on(device((layer + DEPTH - 1) % DEPTH, y, z, c)).wait_recv()

        def near_activations(core):
            for i in range(4):
                activations.part(core, i)

        by_core(c, near_activations)

    def add(old, new):
        return new if old is None else old + new

    def multiply(slots, core, shares=(), weights=True, turned=False):
        products, entries, squares = None, None, None
        for slot in slots:
            k = 2 * slot_z(z, slot) + core
            x = x_ref[slot, core]
            if weights:
                products = add(
                    products, lax.dot_general(x, w_ref[k], TRANSPOSED, preferred_element_type=F32)
                )
            if shares:
                sides = [z_slot(z, 2 * (k % 4)), z_slot(z, 2 * (k % 4) + 1)]
                columns = [
                    jnp.concatenate([u_ref[share, sides[j // 2], j % 2, k // 4] for j in range(4)], 1)
                    for share in shares
                ]
                columns = columns[0] if len(columns) == 1 else jnp.concatenate(columns, 0)
                left, right = (columns, x) if turned else (x, columns)
                entries = add(entries, lax.dot_general(left, right, TRANSPOSED, preferred_element_type=F32))
                wide = x.astype(F32)
                wide = wide * wide
                squares = add(
                    squares, wide[:, :128] + wide[:, 128:256] + wide[:, 256:384] + wide[:, 384:]
                )
        if weights:
            total_ref[...] += products
        if shares:
            if turned:
                inputs_ref[y] += entries
            else:
                every_input_ref[...] += entries
            squares_ref[...] += squares

    def both(numbers, message, between=None, **what):
        def one(i, carry):
            if message is not None:

                @pl.when(i == 1)
                def _():
                    if between is not None:
                        between()
                    activations.from_other(slice(numbers.start, numbers.stop), message)

            multiply(numbers, c + i * (1 - 2 * c), **what)
            return carry

        lax.fori_loop(0, 2, one, 0)

    near, far = range(NEAR.start, NEAR.stop), range(FAR.start, FAR.stop)

    @pl.when(layer == 0)
    def _():
        both(near, 16, shares=[y], turned=True)
        by_core(c, lambda core: activations.part(core, 4))
        both(far, 17, shares=[y], weights=False, turned=True)
        for dy in (2, 1, 3):
            inputs_to(dy).start()
        both(far, None)
        for dy in (1, 3, 2):
            theirs = inputs_ref.at[(y + NY - dy) % NY]
            target = device(layer, (y + dy) % NY, z, c)
            remote(theirs, theirs, inputs_send.at[dy], inputs_recv.at[dy], target).wait_recv()
        for dy in (1, 3, 2):
            inputs_to(dy).wait_send()
        every_input_ref[...] = jnp.concatenate([inputs_ref[i] for i in range(NY)], 0).T

    @pl.when(layer > 0)
    def _():
        hand_far = lambda: by_core(c, lambda core: activations.part(core, 4))
        both(near, 16, between=hand_far, shares=list(range(NY)))
        both(far, 17, shares=list(range(NY)))

    moment = jnp.sum(squares_ref[...], axis=1, keepdims=True) * (UP * UP / FEATURES)
    scale = jnp.where(layer == 0, 1.0, lax.rsqrt(moment + epsilon) * UP)
    inputs = every_input_ref[...]
    inputs_high = inputs.astype(BF16)
    inputs_low = (inputs - inputs_high.astype(F32)).astype(BF16)
    correction = (
        jnp.dot(inputs_high, errors_ref[0], preferred_element_type=F32)
        + jnp.dot(inputs_low, errors_ref[0], preferred_element_type=F32)
        + jnp.dot(inputs_high, errors_ref[1], preferred_element_type=F32)
    )
    output = ((total_ref[...] - correction) * (scale * FEATURES**-0.5)).astype(BF16)
    for q in range(NY):
        out_ref[q] = output[q * QUARTER : (q + 1) * QUARTER]
    scale_ref[...] = jnp.broadcast_to(scale, scale_ref.shape)

    def spread(dy):
        q = (y + dy) % NY
        return remote(
            out_ref.at[q], spread_ref.at[dy], spread_send.at[dy], spread_recv.at[dy], device(layer, q, z, c)
        )

    for dy in (2, 1, 3):
        spread(dy).start()
    residual = x_ref[0, c, my_rows, :].astype(F32) * scale_ref[my_rows, :1]
    combined = residual + silu(out_ref[y].astype(F32))
    for dy in (1, 3, 2):
        spread(dy).wait_recv()
        combined = combined + silu(spread_ref[dy].astype(F32))
    following = device((layer + 1) % DEPTH, y, z, c)

    @pl.when(layer < DEPTH - 1)
    def _():
        hand_ref[...] = (combined * DOWN).astype(BF16)
        hand_on(following).start()

    for p in range(LINE):
        for b in range(4):
            pieces2_ref[p, PAIR * b : PAIR * (b + 1), :] = combined[
                PAIR * p : PAIR * (p + 1), b * 128 : (b + 1) * 128
            ]
    exchange_line(here, pieces2_ref, landed2_ref, act_send, act_recv)
    factor.finish(c)
    by_core(c, activations.finish)
    for dy in (1, 2, 3):
        spread(dy).wait_send()

    @pl.when(source)
    def _():
        for i in range(1, NZ):
            lead_z(i).wait_send()

    @pl.when(y == 0)
    def _():
        for i in range(1, NY):
            lead_y(i).wait_send()

    lead_other(c).wait_send()

    @pl.when(layer < DEPTH - 1)
    def _():
        hand_on(following).wait_send()
    exchange_wait(here, pieces2_ref, landed2_ref, act_send, act_recv)
    pair = landed2_ref[...]
    sums = jnp.sum(jnp.sum(pair * pair, axis=0), axis=1, keepdims=True)
    token = lax.broadcasted_iota(jnp.int32, (PAIR * 4, 1), 0) % PAIR
    mean0 = jnp.sum(jnp.where(token == 0, sums, 0.0), axis=0, keepdims=True) * (1.0 / FEATURES)
    mean1 = jnp.sum(jnp.where(token == 1, sums, 0.0), axis=0, keepdims=True) * (1.0 / FEATURES)
    acts = pair * lax.rsqrt(jnp.where(token == 0, mean0, mean1) + epsilon)[None]
    for p in range(LINE):
        for b in range(4):
            at = p * width + b * 128
            acts_ref[:, at : at + 128] = acts[p, PAIR * b : PAIR * (b + 1), :].astype(BF16)


def forward(tokens, weight, panel, mask):
    width = FEATURES // LINE
    hbm = pl.BlockSpec(memory_space=pl.ANY)
    vmem = pl.BlockSpec(memory_space=pltpu.VMEM)
    dma = pltpu.SemaphoreType.DMA
    return pl.pallas_call(
        forward_kernel,
        out_shape=(
            jax.ShapeDtypeStruct((PAIR, FEATURES), BF16),
            jax.ShapeDtypeStruct((UNITS, LEAD), BF16),
        ),
        in_specs=[hbm] * 4,
        out_specs=(vmem, vmem),
        scratch_shapes=[
            pltpu.VMEM(tokens.shape, BF16),
            pltpu.VMEM(panel.shape, F32),
            pltpu.VMEM(mask.shape, jnp.int32),
            pltpu.VMEM((UNITS, LEAD), BF16),
            pltpu.VMEM((2, LEAD, BLOCK), BF16),
            pltpu.VMEM((LEAD, UNITS), F32),
            pltpu.VMEM((2, LEAD, UNITS), BF16),
            pltpu.VMEM((Z_SLOTS, 2, TOKENS, width), BF16),
            pltpu.VMEM((LINE, UNITS, width), BF16),
            pltpu.VMEM((NY, Z_SLOTS, 2, NY, SHARE, 128), BF16),
            pltpu.VMEM((TOKENS, UNITS), F32),
            pltpu.VMEM((NY, SHARE, TOKENS), F32),
            pltpu.VMEM((TOKENS, LEAD), F32),
            pltpu.VMEM(panel.shape, BF16),
            pltpu.VMEM((TOKENS, 128), F32),
            pltpu.VMEM((TOKENS, 128), F32),
            pltpu.VMEM((NY, QUARTER, UNITS), BF16),
            pltpu.VMEM((NY, QUARTER, UNITS), BF16),
            pltpu.VMEM((QUARTER, UNITS), BF16),
            pltpu.VMEM((LINE, PAIR * 4, 128), F32),
            pltpu.VMEM((LINE, PAIR * 4, 128), F32),
            pltpu.VMEM((LINE, PAIR * 4, 128), F32),
            pltpu.VMEM((LINE, PAIR * 4, 128), F32),
            dma((LINE + 4,)),
            dma((12,)),
            dma((12,)),
            dma,
            dma,
            dma,
            dma,
            dma((7,)),
            dma((7,)),
            dma((NY,)),
            dma((NY,)),
            dma((NY,)),
            dma((NY,)),
            dma,
            dma,
            *GATHER_SEMS,
            *GATHER_SEMS,
        ],
        compiler_params=pltpu.CompilerParams(
            collective_id=0, has_side_effects=True, vmem_limit_bytes=60 * 2**20
        ),
        name="forward",
    )(tokens, weight, panel, mask)


def hand_out_kernel(acts_in, pruned_in, acts_out, pruned_out):
    acts_out[...] = acts_in[...]
    pruned_out[...] = pruned_in[...]


def hand_out(acts, pruned):
    vmem = pl.BlockSpec(memory_space=pltpu.VMEM)
    return pl.pallas_call(
        hand_out_kernel,
        out_shape=(
            jax.ShapeDtypeStruct(acts.shape, acts.dtype),
            jax.ShapeDtypeStruct(pruned.shape, pruned.dtype),
        ),
        in_specs=[vmem, vmem],
        out_specs=(vmem, vmem),
        name="hand_out",
    )(acts, pruned)


def per_device(tokens, up_weight, hess_panel, keep_mask):
    acts, pruned = hand_out(*forward(tokens, up_weight[0], hess_panel[0], keep_mask[0]))
    return (acts[None], pruned[None])


def solution(mesh):
    in_specs = (
        P("row", None),
        P("layer", "row", None),
        P("layer", None, "row"),
        P("layer", "row", None),
    )
    out_specs = (P("layer", "row", None), P("layer", "row", None))
    return jax.shard_map(
        per_device, mesh=mesh, in_specs=in_specs, out_specs=out_specs, check_vma=False
    )
```
